32 devices in a mesh: slab: 16 (over z, y, x), tile: 2 (over core).
Axes of the slice: x: 2, y: 2, z: 4, core: 2. Of those that a mesh axis runs over, the one named last changes fastest.
Arguments:
- samples: float32 [16, 64, 32, 256], P('slab', None, 'tile'), may hold values from -6 to 6
- counts: int32 [16, 64, 32], P('slab', None, 'tile'), may hold values from 1 to 4
- w_in: float32 [16, 64, 256], P('slab'), may hold values from -0.75 to 0.75
- b_in: float32 [16, 256], P('slab'), may hold values from -3 to 3
- w_color: float32 [16, 256, 128], P('slab'), may hold values from -0.375 to 0.375
- b_color: float32 [16, 128], P('slab'), may hold values from -3 to 3
- w_density: float32 [16, 256], P('slab'), may hold values from -0.375 to 0.375
- b_density: float32 [16], P('slab'), may hold values from -1 to 1
- conv_a: bfloat16 [3, 3, 128, 128], replicated, may hold values from -0.1875 to 0.1875
- bias_a: float32 [128], replicated, may hold values from -3 to 3
- conv_b: bfloat16 [3, 3, 128, 128], replicated, may hold values from -0.1875 to 0.1875
- bias_b: float32 [128], replicated, may hold values from -3 to 3
Outputs:
- decoded: bfloat16 [64, 32, 128], P('slab', 'tile')
- front: float32 [16, 64, 32], P('slab', None, 'tile')
The draws below stay inside these ranges and needn't reach their ends.
All inputs are finite; a program needn't handle non-finite values.
Results may differ from the reference program's by a relative error of at most 0.006.
Values may be sent and summed in bfloat16 or wider, within the bound.
A program may use at most 128 MiB of HBM per device.

```python
import jax
import jax.numpy as jnp
from jax import lax

F = 64
HID = 256
C = 128
K = 4
STRIP = 4
SLABS = 16
HEIGHT = 64
WIDTH = 32


def place_ends(array, stream_key, least, largest):
    longest = array.shape.index(max(array.shape))
    spots = []
    for shift in (0, 1):
        where = [jax.random.randint(jax.random.fold_in(stream_key, axis), (), 0, length) for axis, length in enumerate(array.shape)]
        where[longest] = (where[longest] + shift) % array.shape[longest]
        spots.append(tuple(where))
    return array.at[spots[0]].set(least).at[spots[1]].set(largest)


def steps_of(own_key, dims, cuts, smallest, top_value):
    def one(axis_at, shards_of):
        steps = jax.random.uniform(jax.random.fold_in(jax.random.fold_in(own_key, 6), axis_at), (shards_of,), jnp.float32, smallest / len(cuts), top_value / len(cuts))
        return jnp.repeat(jnp.exp(steps), dims[axis_at] // shards_of).reshape((-1,) + (1,) * (len(dims) - axis_at - 1))

    gain = one(*cuts[0])
    for cut in cuts[1:]:
        gain = gain * one(*cut)
    return gain


def gaussian(stream_key, dims, spread, reach, cuts=(), held_as=jnp.bfloat16):
    factor_of = steps_of(stream_key, dims, cuts, -0.22, 0.18) if cuts else 1.0
    entries = jax.random.normal(stream_key, dims, jnp.float32) * spread * factor_of
    return jnp.minimum(jnp.maximum(entries, -reach), reach).astype(held_as)


def setup_inputs(seed: int = 0) -> dict:
    arg_keys = jax.random.split(jax.random.key(seed), 13)
    return {
        "samples": gaussian(arg_keys[0], (SLABS, HEIGHT, WIDTH, K * F), 1.0, 6.0, ((0, 16), (2, 2)), jnp.float32),
        "counts": place_ends(jax.random.randint(arg_keys[1], (SLABS, HEIGHT, WIDTH), 1, K + 1), jax.random.fold_in(arg_keys[1], 1), 1, K).astype(jnp.int32),
        "w_in": gaussian(arg_keys[2], (SLABS, F, HID), F ** -0.5, 0.75, ((0, 16),), jnp.float32),
        "b_in": gaussian(arg_keys[3], (SLABS, HID), 0.5, 3.0, ((0, 16),), jnp.float32),
        "w_color": gaussian(arg_keys[4], (SLABS, HID, C), HID ** -0.5, 0.375, ((0, 16),), jnp.float32),
        "b_color": gaussian(arg_keys[5], (SLABS, C), 0.5, 3.0, ((0, 16),), jnp.float32),
        "w_density": gaussian(arg_keys[6], (SLABS, HID), HID ** -0.5, 0.375, ((0, 16),), jnp.float32),
        "b_density": jnp.clip(jax.random.uniform(arg_keys[7], (SLABS,), jnp.float32, -1.0, 1.0) * steps_of(arg_keys[7], (SLABS,), ((0, 16),), -0.4, 0.0), -1.0, 1.0),
        "conv_a": gaussian(arg_keys[8], (3, 3, C, C), (9 * C) ** -0.5, 0.1875),
        "bias_a": gaussian(arg_keys[9], (C,), 0.5, 3.0, (), jnp.float32),
        "conv_b": gaussian(arg_keys[10], (3, 3, C, C), (9 * C) ** -0.5, 0.1875),
        "bias_b": gaussian(arg_keys[11], (C,), 0.5, 3.0, (), jnp.float32),
    }


def hidden_units(inputs, w_in, b_in):
    shaped = inputs.reshape(inputs.shape[:-1] + (K, F))
    return jax.nn.relu(jnp.einsum('rwkf,fh->rwkh', shaped, w_in, precision=lax.Precision.HIGHEST) + b_in)


def densities(hidden_act, w_density, b_density, live_count):
    before = jnp.einsum('rwkh,h->rwk', hidden_act, w_density, precision=lax.Precision.HIGHEST) + b_density
    slots = lax.broadcasted_iota(jnp.int32, before.shape, 2)
    return jnp.where(slots < live_count[..., None], jax.nn.softplus(before), 0.0)


def sample_weights(density, front, total):
    scaled = density / total[..., None]
    earlier = jnp.cumsum(scaled, axis=2) - scaled
    return jnp.exp(-front[..., None] - earlier) * (1.0 - jnp.exp(-scaled))


def partial_image(hidden_act, weight, w_color, b_color):
    color = jnp.einsum('rwkh,hc->rwkc', hidden_act, w_color, precision=lax.Precision.HIGHEST) + b_color
    return jnp.einsum('rwk,rwkc->rwc', weight, color, precision=lax.Precision.HIGHEST)


def convolve(image, kernel):
    result = lax.conv_general_dilated(image.astype(jnp.float32)[None], kernel.astype(jnp.float32), (1, 1), 'SAME',
                                      dimension_numbers=('NHWC', 'HWIO', 'NHWC'), precision=lax.Precision.HIGHEST)
    return result[0]


def reference(samples, counts, w_in, b_in, w_color, b_color, w_density, b_density, conv_a, bias_a, conv_b, bias_b):
    blocks = HEIGHT // STRIP

    def slab_density(packed):
        inputs, live, first_w, first_b, dens_w, dens_b = packed

        def per_block(pair):
            return densities(hidden_units(pair[0], first_w, first_b), dens_w, dens_b, pair[1])

        pieces = lax.map(per_block, (inputs.reshape(blocks, STRIP, WIDTH, K * F), live.reshape(blocks, STRIP, WIDTH)))
        return pieces.reshape(HEIGHT, WIDTH, K)

    density = lax.map(slab_density, (samples, counts, w_in, b_in, w_density, b_density))
    depth = jnp.sum(density, axis=3)
    total = jnp.sum(depth, axis=0)
    prefix = jnp.cumsum(depth, axis=0) - depth
    front = prefix / total

    def add_slab(image, packed):
        inputs, dens, ahead, first_w, first_b, col_w, col_b = packed
        weight = sample_weights(dens, ahead, total)

        def per_block(pair):
            return partial_image(hidden_units(pair[0], first_w, first_b), pair[1], col_w, col_b)

        part = lax.map(per_block, (inputs.reshape(blocks, STRIP, WIDTH, K * F), weight.reshape(blocks, STRIP, WIDTH, K)))
        return image + part.reshape(HEIGHT, WIDTH, C), None

    start_image = jnp.zeros((HEIGHT, WIDTH, C), jnp.float32)
    image, _ = lax.scan(add_slab, start_image, (samples, density, front, w_in, b_in, w_color, b_color))
    image = image.astype(jnp.bfloat16)
    hidden_map = jax.nn.relu(convolve(image, conv_a) + bias_a).astype(jnp.bfloat16)
    decoded = (convolve(hidden_map, conv_b) + bias_b).astype(jnp.bfloat16)
    return (decoded, front)
```

```python
import functools

import jax
import jax.numpy as jnp
from jax import lax
from jax.experimental import pallas as pl
from jax.experimental.pallas import tpu as pltpu
from jax.sharding import PartitionSpec as P

F = 64
K = 4
LANES = 128
MESH = pl.DeviceIdType.MESH
BF16 = jnp.bfloat16
F32 = jnp.float32


def dot(a, b):
    return jnp.dot(a, b, preferred_element_type=F32)


def render_kernel(
    slabs,
    samples_hbm,
    counts_ref,
    w_in_hbm,
    b_in_ref,
    w_color_hbm,
    b_color_ref,
    w_density_ref,
    b_density_ref,
    conv_a_hbm,
    bias_a_ref,
    conv_b_hbm,
    bias_b_ref,
    decoded_ref,
    front_ref,
    samples_ref,
    w_in_ref,
    w_color_ref,
    conv_a_ref,
    conv_b_ref,
    taps_a,
    taps_b,
    density_ref,
    colors_ref,
    weight_ref,
    depths_ref,
    sent_ref,
    parts_ref,
    field_ref,
    load_sems,
    depth_send,
    depth_recv,
    part_send,
    part_recv,
    edge_send,
    edge_recv,
):
    me = lax.axis_index("slab")
    tile = lax.axis_index("tile")
    other = 1 - tile
    rows, cols = samples_ref.shape[0], samples_ref.shape[1]
    groups = rows * cols // LANES
    group_rows = LANES // cols
    strip = rows // slabs
    strip_rays = strip * cols
    hid = w_in_ref.shape[1]
    channels = w_color_ref.shape[1]
    not_first = me > 0
    not_last = me < slabs - 1

    loads = [
        pltpu.make_async_copy(src, dst, load_sems.at[i])
        for i, (src, dst) in enumerate(
            (
                (w_in_hbm.at[0], w_in_ref),
                (samples_hbm.at[0], samples_ref),
                (w_color_hbm.at[0], w_color_ref),
                (conv_a_hbm, conv_a_ref),
                (conv_b_hbm, conv_b_ref),
            )
        )
    ]
    for load in loads:
        load.start()

    barrier = pltpu.get_barrier_semaphore()

    def greet(slab, tile_at):
        pl.semaphore_signal(barrier, inc=1, device_id=(slab, tile_at), device_id_type=MESH)

    def greet_slab(shift, carry):
        greet(lax.rem(me + shift, slabs), tile)
        return carry

    lax.fori_loop(1, slabs, greet_slab, 0)
    greet(me, other)

    @pl.when(not_first)
    def _():
        greet(me - 1, other)

    @pl.when(not_last)
    def _():
        greet(me + 1, other)

    eye = lax.broadcasted_iota(jnp.int32, (LANES, LANES), 0) == lax.broadcasted_iota(
        jnp.int32, (LANES, LANES), 1
    )

    loads[0].wait()
    w_in = w_in_ref[...]
    high = w_in.astype(BF16)
    low = (w_in - high.astype(F32)).astype(BF16)
    blank = jnp.zeros_like(high)
    even = [high, blank, high, blank, low, blank]
    odd = [blank, high, blank, high, blank, low]
    pair_w = jnp.concatenate(
        [jnp.concatenate(even, axis=0), jnp.concatenate(odd, axis=0)], axis=1
    )
    pair_b = jnp.concatenate([b_in_ref[...], b_in_ref[...]], axis=1)
    loads[2].wait()
    density_cols = jnp.transpose(jnp.broadcast_to(w_density_ref[...], (LANES, hid)))
    heads = jnp.concatenate([w_color_ref[...].astype(BF16), density_cols.astype(BF16)], axis=1)
    b_color = b_color_ref[...]
    loads[1].wait()
    chunk = 2
    for c in range(groups // chunk):
        rays = chunk * LANES
        x = samples_ref[c * chunk * group_rows : (c + 1) * chunk * group_rows].reshape(rays, K * F)
        for pair in range(K // 2):
            part = x[:, pair * LANES : (pair + 1) * LANES]
            part_high = part.astype(BF16)
            part_low = (part - part_high.astype(F32)).astype(BF16)
            both = jnp.concatenate([part_high, part_low, part_high], axis=1)
            act = jnp.maximum(dot(both, pair_w) + pair_b, 0.0).astype(BF16)
            for half in range(2):
                k = 2 * pair + half
                out = dot(act[:, half * hid : (half + 1) * hid], heads)
                color = (out[:, :channels] + b_color).astype(BF16)
                before = out[:, channels:].reshape(chunk, LANES, LANES)
                for g in range(chunk):
                    colors_ref[c * chunk + g, k * LANES : (k + 1) * LANES, :] = color[
                        g * LANES : (g + 1) * LANES
                    ]
                density_ref[k, c * chunk : (c + 1) * chunk, :] = jnp.sum(
                    jnp.where(eye, before, 0.0), axis=1
                )

    spread = (
        lax.rem(lax.broadcasted_iota(jnp.int32, (cols, LANES), 1), cols)
        == lax.broadcasted_iota(jnp.int32, (cols, LANES), 0)
    ).astype(BF16)
    own_lane = (
        lax.broadcasted_iota(jnp.int32, (group_rows, LANES), 1) // cols
        == lax.broadcasted_iota(jnp.int32, (group_rows, LANES), 0)
    )
    live = dot(counts_ref[0].astype(F32).astype(BF16), spread).reshape(groups, group_rows, LANES)
    live = jnp.sum(jnp.where(own_lane, live, 0.0), axis=1)

    density = []
    for k in range(K):
        z = density_ref[k] + b_density_ref[0]
        soft = jnp.maximum(z, 0.0) + jnp.log1p(jnp.exp(-jnp.abs(z)))
        density.append(jnp.where(live > k, soft, 0.0))
    depths_ref[me] = density[0] + density[1] + density[2] + density[3]

    pl.semaphore_wait(
        barrier, slabs + not_first.astype(jnp.int32) + not_last.astype(jnp.int32)
    )

    def send_depth(shift, carry):
        pltpu.make_async_remote_copy(
            src_ref=depths_ref.at[me],
            dst_ref=depths_ref.at[me],
            send_sem=depth_send,
            recv_sem=depth_recv,
            device_id=(lax.rem(me + shift, slabs), tile),
            device_id_type=MESH,
        ).start()
        return carry

    lax.fori_loop(1, slabs, send_depth, 0)

    loads[3].wait()
    loads[4].wait()
    for taps, conv in ((taps_a, conv_a_ref), (taps_b, conv_b_ref)):
        for r in range(3):
            for s in range(3):
                taps[r * channels : (r + 1) * channels, s * channels : (s + 1) * channels] = conv[
                    r, s
                ]

    peers = depths_ref.at[pl.ds(0, slabs - 1)]
    pltpu.make_async_copy(peers, peers, depth_recv).wait()
    total = depths_ref[0]
    prefix = jnp.where(me > 0, depths_ref[0], 0.0)
    for s in range(1, slabs):
        one = depths_ref[s]
        total = total + one
        prefix = prefix + jnp.where(s < me, one, 0.0)
    front = prefix / total
    ahead = front
    for k in range(K):
        scaled = density[k] / total
        weight_ref[k] = jnp.exp(-ahead) * (1.0 - jnp.exp(-scaled))
        ahead = ahead + scaled

    def send_part(owner):
        pltpu.make_async_remote_copy(
            src_ref=sent_ref.at[owner],
            dst_ref=parts_ref.at[me],
            send_sem=part_send,
            recv_sem=part_recv,
            device_id=(owner, tile),
            device_id_type=MESH,
        ).start()

    strips = LANES // strip_rays
    place = lax.rem(me, strips)
    for i in range(groups):
        g = lax.rem(me // strips + i, groups)
        diag = [
            jnp.where(eye, weight_ref[k, pl.ds(g, 1), :], 0.0).astype(BF16) for k in range(K)
        ]
        image = dot(jnp.concatenate(diag, axis=1), colors_ref[g]).astype(BF16)
        sent_ref[pl.ds(strips * g, strips)] = image.reshape(strips, strip_rays, channels)
        for j in range(strips):
            if i > 0:
                send_part(strips * g + j)
            elif j > 0:
                send_part(strips * g + lax.rem(place + j, strips))
    parts_ref[me] = sent_ref[me]

    laid = jnp.where(own_lane, front[:, None, :], 0.0).reshape(rows, LANES)
    gather = (
        lax.rem(lax.broadcasted_iota(jnp.int32, (LANES, cols), 0), cols)
        == lax.broadcasted_iota(jnp.int32, (LANES, cols), 1)
    ).astype(BF16)
    first = laid.astype(BF16)
    rest = laid - first.astype(F32)
    second = rest.astype(BF16)
    third = (rest - second.astype(F32)).astype(BF16)
    front_ref[0] = dot(first, gather) + dot(second, gather) + dot(third, gather)

    peers = parts_ref.at[pl.ds(0, slabs - 1)]
    pltpu.make_async_copy(peers, peers, part_recv).wait()
    image = parts_ref[0].astype(F32)
    for s in range(1, slabs):
        image = image + parts_ref[s].astype(F32)
    image = image.astype(BF16).reshape(strip, cols, channels)

    field_ref[0, 2 : 2 + strip] = image
    edge = jnp.zeros((2, 2, cols, channels), BF16)

    def edge_copy(which, source, target, device):
        return pltpu.make_async_remote_copy(
            src_ref=source,
            dst_ref=target,
            send_sem=edge_send.at[which],
            recv_sem=edge_recv.at[which],
            device_id=device,
            device_id_type=MESH,
        )

    own = field_ref.at[0, pl.ds(2, strip)]
    head = field_ref.at[0, pl.ds(2, 2)]
    tail = field_ref.at[0, pl.ds(strip, 2)]
    up = [
        edge_copy(1, head, field_ref.at[0, pl.ds(strip + 2, 2)], (me - 1, tile)),
        edge_copy(2, head, field_ref.at[1, pl.ds(strip + 2, 2)], (me - 1, other)),
    ]
    down = [
        edge_copy(3, tail, field_ref.at[0, pl.ds(0, 2)], (me + 1, tile)),
        edge_copy(4, tail, field_ref.at[1, pl.ds(0, 2)], (me + 1, other)),
    ]
    across = edge_copy(0, own, field_ref.at[1, pl.ds(2, strip)], (me, other))

    @pl.when(not_first)
    def _():
        for copy in up:
            copy.start()

    @pl.when(not_last)
    def _():
        for copy in down:
            copy.start()

    across.start()

    @pl.when(jnp.logical_not(not_first))
    def _():
        field_ref[:, 0:2] = edge

    @pl.when(jnp.logical_not(not_last))
    def _():
        field_ref[:, strip + 2 : strip + 4] = edge

    @pl.when(not_last)
    def _():
        for copy in up:
            copy.wait_recv()

    @pl.when(not_first)
    def _():
        for copy in down:
            copy.wait_recv()

    across.wait_recv()

    place = lax.broadcasted_iota(jnp.int32, (1, cols, 1), 1)
    near = jnp.where(tile == 0, place, cols - 1 - place) < 2
    side = jnp.where(near, field_ref[1].astype(F32), 0.0).astype(BF16)
    ring = jnp.concatenate([field_ref[0], side], axis=1)

    def convolve(cells, taps, bias):
        out_rows = cells.shape[0] - 2
        span = cells.shape[1]
        stacked = jnp.concatenate(
            [cells[r : r + out_rows].reshape(out_rows * span, channels) for r in range(3)], axis=1
        )
        shifted = dot(stacked, taps[...]).reshape(out_rows, span, 3 * channels)
        return (
            pltpu.roll(shifted[:, :, :channels], 1, 1)
            + shifted[:, :, channels : 2 * channels]
            + pltpu.roll(shifted[:, :, 2 * channels :], span - 1, 1)
            + bias
        )

    hidden_map = jnp.maximum(convolve(ring, taps_a, bias_a_ref[...].reshape(1, 1, channels)), 0.0)
    shape = (strip + 2, 2 * cols, 1)
    at_row = lax.broadcasted_iota(jnp.int32, shape, 0) + me * strip - 1
    at_col = lax.broadcasted_iota(jnp.int32, shape, 1)
    in_rows = jnp.logical_and(at_row >= 0, at_row < rows)
    outside = jnp.where(tile == 0, 2 * cols - 1, cols)
    hidden_map = jnp.where(jnp.logical_and(in_rows, at_col != outside), hidden_map, 0.0)
    decoded = convolve(hidden_map.astype(BF16), taps_b, bias_b_ref[...].reshape(1, 1, channels))
    decoded_ref[...] = decoded[:, :cols].astype(BF16)

    peers = depths_ref.at[pl.ds(0, slabs - 1)]
    pltpu.make_async_copy(peers, peers, depth_send).wait()
    peers = parts_ref.at[pl.ds(0, slabs - 1)]
    pltpu.make_async_copy(peers, peers, part_send).wait()
    across.wait_send()

    @pl.when(not_first)
    def _():
        for copy in up:
            copy.wait_send()

    @pl.when(not_last)
    def _():
        for copy in down:
            copy.wait_send()


def body(
    slabs,
    samples,
    counts,
    w_in,
    b_in,
    w_color,
    b_color,
    w_density,
    b_density,
    conv_a,
    bias_a,
    conv_b,
    bias_b,
):
    _, rows, cols, width = samples.shape
    hid, channels = w_color.shape[1:]
    groups = rows * cols // LANES
    strip = rows // slabs
    vmem = pl.BlockSpec(memory_space=pltpu.VMEM)
    smem = pl.BlockSpec(memory_space=pltpu.SMEM)
    hbm = pl.BlockSpec(memory_space=pl.ANY)
    dma = pltpu.SemaphoreType.DMA
    return pl.pallas_call(
        functools.partial(render_kernel, slabs),
        out_shape=(
            jax.ShapeDtypeStruct((strip, cols, channels), BF16),
            jax.ShapeDtypeStruct((1, rows, cols), F32),
        ),
        in_specs=[hbm, vmem, hbm, vmem, hbm, vmem, vmem, smem, hbm, vmem, hbm, vmem],
        out_specs=(vmem, vmem),
        scratch_shapes=[
            pltpu.VMEM((rows, cols, width), F32),
            pltpu.VMEM(w_in.shape[1:], F32),
            pltpu.VMEM(w_color.shape[1:], F32),
            pltpu.VMEM(conv_a.shape, BF16),
            pltpu.VMEM(conv_b.shape, BF16),
            pltpu.VMEM((3 * channels, 3 * channels), BF16),
            pltpu.VMEM((3 * channels, 3 * channels), BF16),
            pltpu.VMEM((K, groups, LANES), F32),
            pltpu.VMEM((groups, K * LANES, channels), BF16),
            pltpu.VMEM((K, groups, LANES), F32),
            pltpu.VMEM((slabs, groups, LANES), F32),
            pltpu.VMEM((slabs, strip * cols, channels), BF16),
            pltpu.VMEM((slabs, strip * cols, channels), BF16),
            pltpu.VMEM((2, strip + 4, cols, channels), BF16),
            dma((5,)),
            dma,
            dma,
            dma,
            dma,
            dma((5,)),
            dma((5,)),
        ],
        compiler_params=pltpu.CompilerParams(
            collective_id=0, has_side_effects=True, vmem_limit_bytes=40 * 2**20
        ),
    )(
        samples,
        counts,
        w_in,
        b_in,
        w_color,
        b_color,
        w_density,
        b_density,
        conv_a,
        bias_a.reshape(1, channels),
        conv_b,
        bias_b.reshape(1, channels),
    )


def solution(mesh):
    in_specs = (
        P("slab", None, "tile", None),
        P("slab", None, "tile"),
        P("slab", None, None),
        P("slab", None),
        P("slab", None, None),
        P("slab", None),
        P("slab", None),
        P("slab"),
        P(),
        P(),
        P(),
        P(),
    )
    out_specs = (P("slab", "tile", None), P("slab", None, "tile"))
    run = functools.partial(body, mesh.shape["slab"])
    return jax.shard_map(run, mesh=mesh, in_specs=in_specs, out_specs=out_specs, check_vma=False)
```

```python
import functools

import jax
import jax.numpy as jnp
from jax import lax
from jax.experimental import pallas as pl
from jax.experimental.pallas import tpu as pltpu
from jax.sharding import PartitionSpec as P

F = 64
K = 4
LANES = 128
MESH = pl.DeviceIdType.MESH
BF16 = jnp.bfloat16
F32 = jnp.float32


def dot(a, b):
    return jnp.dot(a, b, preferred_element_type=F32)


def dot_last(a, b):
    return lax.dot_general(a, b, (((1,), (1,)), ((), ())), preferred_element_type=F32)


def render_kernel(
    slabs,
    samples_hbm,
    counts_hbm,
    w_in_hbm,
    b_in_hbm,
    w_color_hbm,
    b_color_hbm,
    w_density_hbm,
    b_density_ref,
    conv_a_hbm,
    bias_a_hbm,
    conv_b_hbm,
    bias_b_hbm,
    decoded_ref,
    front_ref,
    samples_ref,
    counts_ref,
    w_in_ref,
    b_in_ref,
    w_color_ref,
    b_color_ref,
    w_density_ref,
    conv_a_ref,
    bias_a_ref,
    conv_b_ref,
    bias_b_ref,
    taps_a,
    taps_b,
    density_ref,
    colors_ref,
    weight_ref,
    depths_ref,
    sent_ref,
    parts_ref,
    field_ref,
    load_sems,
    depth_send,
    depth_recv,
    part_send,
    part_recv,
    edge_send,
    edge_recv,
):
    me = lax.axis_index("slab")
    tile = lax.axis_index("tile")
    other = 1 - tile
    rows, cols = samples_ref.shape[0], samples_ref.shape[1]
    groups = rows * cols // LANES
    group_rows = LANES // cols
    strip = rows // slabs
    strip_rays = strip * cols
    hid = w_in_ref.shape[1]
    channels = w_color_ref.shape[1]
    not_first = me > 0
    not_last = me < slabs - 1

    chunk = 2
    chunk_rows = chunk * group_rows
    pieces = [pl.ds(i * chunk_rows, chunk_rows) for i in range(groups // chunk)]
    first_loads = [
        (w_in_hbm.at[0], w_in_ref),
        (b_in_hbm, b_in_ref),
        (w_color_hbm.at[0], w_color_ref),
        (w_density_hbm, w_density_ref),
        (b_color_hbm, b_color_ref),
    ]
    last_loads = [
        (counts_hbm.at[0], counts_ref),
        (conv_a_hbm, conv_a_ref),
        (conv_b_hbm, conv_b_ref),
        (bias_a_hbm, bias_a_ref),
        (bias_b_hbm, bias_b_ref),
    ]
    sample_loads = [(samples_hbm.at[0, piece], samples_ref.at[piece]) for piece in pieces]
    loads = [
        pltpu.make_async_copy(src, dst, load_sems.at[i])
        for i, (src, dst) in enumerate(first_loads + last_loads + sample_loads)
    ]
    sample_loads = loads[len(first_loads) + len(last_loads) :]
    last_loads = loads[len(first_loads) : len(first_loads) + len(last_loads)]
    first_loads = loads[: len(first_loads)]
    for load in first_loads + sample_loads + last_loads:
        load.start()

    barrier = pltpu.get_barrier_semaphore()

    def greet(slab, tile_at):
        pl.semaphore_signal(barrier, inc=1, device_id=(slab, tile_at), device_id_type=MESH)

    def greet_slab(shift, carry):
        greet(lax.rem(me + shift, slabs), tile)
        return carry

    lax.fori_loop(1, slabs, greet_slab, 0)
    greet(me, other)

    @pl.when(not_first)
    def _():
        greet(me - 1, other)

    @pl.when(not_last)
    def _():
        greet(me + 1, other)

    eye = lax.broadcasted_iota(jnp.int32, (LANES, LANES), 0) == lax.broadcasted_iota(
        jnp.int32, (LANES, LANES), 1
    )

    for load in first_loads:
        load.wait()
    w_in = w_in_ref[...]
    high = w_in.astype(BF16)
    low = (w_in - high.astype(F32)).astype(BF16)
    blank = jnp.zeros_like(high)
    even = [high, blank, high, blank, low, blank]
    odd = [blank, high, blank, high, blank, low]
    pair_w = jnp.concatenate(
        [jnp.concatenate(even, axis=0), jnp.concatenate(odd, axis=0)], axis=1
    )
    pair_b = jnp.concatenate([b_in_ref[...], b_in_ref[...]], axis=1)
    density_cols = jnp.transpose(jnp.broadcast_to(w_density_ref[...], (LANES, hid)))
    heads = jnp.concatenate([w_color_ref[...].astype(BF16), density_cols.astype(BF16)], axis=1)
    b_color = b_color_ref[...]
    for c in range(groups // chunk):
        rays = chunk * LANES
        sample_loads[c].wait()
        x = samples_ref[c * chunk * group_rows : (c + 1) * chunk * group_rows].reshape(rays, K * F)
        for pair in range(K // 2):
            part = x[:, pair * LANES : (pair + 1) * LANES]
            part_high = part.astype(BF16)
            part_low = (part - part_high.astype(F32)).astype(BF16)
            both = jnp.concatenate([part_high, part_low, part_high], axis=1)
            act = jnp.maximum(dot(both, pair_w) + pair_b, 0.0).astype(BF16)
            for half in range(2):
                k = 2 * pair + half
                out = dot(act[:, half * hid : (half + 1) * hid], heads)
                color = (out[:, :channels] + b_color).astype(BF16)
                before = out[:, channels:].reshape(chunk, LANES, LANES)
                for g in range(chunk):
                    colors_ref[c * chunk + g, k * LANES : (k + 1) * LANES, :] = color[
                        g * LANES : (g + 1) * LANES
                    ]
                density_ref[k, c * chunk : (c + 1) * chunk, :] = jnp.sum(
                    jnp.where(eye, before, 0.0), axis=1
                )

    for load in last_loads:
        load.wait()

    spread = (
        lax.rem(lax.broadcasted_iota(jnp.int32, (cols, LANES), 1), cols)
        == lax.broadcasted_iota(jnp.int32, (cols, LANES), 0)
    ).astype(BF16)
    own_lane = (
        lax.broadcasted_iota(jnp.int32, (group_rows, LANES), 1) // cols
        == lax.broadcasted_iota(jnp.int32, (group_rows, LANES), 0)
    )
    row_eye = (
        lax.broadcasted_iota(jnp.int32, (rows, rows), 0)
        == lax.broadcasted_iota(jnp.int32, (rows, rows), 1)
    ).astype(BF16)
    by_row = dot_last(row_eye, counts_ref[...].astype(F32).astype(BF16)).astype(BF16)
    live = dot(by_row, spread).reshape(groups, group_rows, LANES)
    live = jnp.sum(jnp.where(own_lane, live, 0.0), axis=1)

    density = []
    for k in range(K):
        z = density_ref[k] + b_density_ref[0]
        soft = jnp.maximum(z, 0.0) + jnp.log1p(jnp.exp(-jnp.abs(z)))
        density.append(jnp.where(live > k, soft, 0.0))
    depths_ref[me] = density[0] + density[1] + density[2] + density[3]

    pl.semaphore_wait(
        barrier, slabs + not_first.astype(jnp.int32) + not_last.astype(jnp.int32)
    )

    def send_depth(shift, carry):
        pltpu.make_async_remote_copy(
            src_ref=depths_ref.at[me],
            dst_ref=depths_ref.at[me],
            send_sem=depth_send,
            recv_sem=depth_recv,
            device_id=(lax.rem(me + shift, slabs), tile),
            device_id_type=MESH,
        ).start()
        return carry

    lax.fori_loop(1, slabs, send_depth, 0)

    for taps, conv in ((taps_a, conv_a_ref), (taps_b, conv_b_ref)):
        for r in range(3):
            for s in range(3):
                taps[r * channels : (r + 1) * channels, s * channels : (s + 1) * channels] = conv[
                    r, s
                ]

    peers = depths_ref.at[pl.ds(0, slabs - 1)]
    pltpu.make_async_copy(peers, peers, depth_recv).wait()
    total = depths_ref[0]
    prefix = jnp.where(me > 0, depths_ref[0], 0.0)
    for s in range(1, slabs):
        one = depths_ref[s]
        total = total + one
        prefix = prefix + jnp.where(s < me, one, 0.0)
    front = prefix / total
    ahead = front
    for k in range(K):
        scaled = density[k] / total
        weight_ref[k] = jnp.exp(-ahead) * (1.0 - jnp.exp(-scaled))
        ahead = ahead + scaled

    def send_part(owner):
        pltpu.make_async_remote_copy(
            src_ref=sent_ref.at[owner],
            dst_ref=parts_ref.at[me],
            send_sem=part_send,
            recv_sem=part_recv,
            device_id=(owner, tile),
            device_id_type=MESH,
        ).start()

    strips = LANES // strip_rays
    place = lax.rem(me, strips)
    for i in range(groups):
        g = lax.rem(me // strips + i, groups)
        diag = [
            jnp.where(eye, weight_ref[k, pl.ds(g, 1), :], 0.0).astype(BF16) for k in range(K)
        ]
        image = dot(jnp.concatenate(diag, axis=1), colors_ref[g]).astype(BF16)
        sent_ref[pl.ds(strips * g, strips)] = image.reshape(strips, strip_rays, channels)
        for j in range(strips):
            if i > 0:
                send_part(strips * g + j)
            elif j > 0:
                send_part(strips * g + lax.rem(place + j, strips))
    parts_ref[me] = sent_ref[me]

    laid = jnp.where(own_lane, front[:, None, :], 0.0).reshape(rows, LANES)
    first = laid.astype(BF16)
    rest = laid - first.astype(F32)
    second = rest.astype(BF16)
    third = (rest - second.astype(F32)).astype(BF16)
    front_ref[0] = dot_last(spread, first) + dot_last(spread, second) + dot_last(spread, third)

    peers = parts_ref.at[pl.ds(0, slabs - 1)]
    pltpu.make_async_copy(peers, peers, part_recv).wait()
    image = parts_ref[0].astype(F32)
    for s in range(1, slabs):
        image = image + parts_ref[s].astype(F32)
    image = image.astype(BF16).reshape(strip, cols, channels)

    field_ref[0, 2 : 2 + strip] = image
    edge = jnp.zeros((2, 2, cols, channels), BF16)

    def edge_copy(which, source, target, device):
        return pltpu.make_async_remote_copy(
            src_ref=source,
            dst_ref=target,
            send_sem=edge_send.at[which],
            recv_sem=edge_recv.at[which],
            device_id=device,
            device_id_type=MESH,
        )

    own = field_ref.at[0, pl.ds(2, strip)]
    head = field_ref.at[0, pl.ds(2, 2)]
    tail = field_ref.at[0, pl.ds(strip, 2)]
    up = [
        edge_copy(1, head, field_ref.at[0, pl.ds(strip + 2, 2)], (me - 1, tile)),
        edge_copy(2, head, field_ref.at[1, pl.ds(strip + 2, 2)], (me - 1, other)),
    ]
    down = [
        edge_copy(3, tail, field_ref.at[0, pl.ds(0, 2)], (me + 1, tile)),
        edge_copy(4, tail, field_ref.at[1, pl.ds(0, 2)], (me + 1, other)),
    ]
    across = edge_copy(0, own, field_ref.at[1, pl.ds(2, strip)], (me, other))

    @pl.when(not_first)
    def _():
        for copy in up:
            copy.start()

    @pl.when(not_last)
    def _():
        for copy in down:
            copy.start()

    across.start()

    @pl.when(jnp.logical_not(not_first))
    def _():
        field_ref[:, 0:2] = edge

    @pl.when(jnp.logical_not(not_last))
    def _():
        field_ref[:, strip + 2 : strip + 4] = edge

    @pl.when(not_last)
    def _():
        for copy in up:
            copy.wait_recv()

    @pl.when(not_first)
    def _():
        for copy in down:
            copy.wait_recv()

    across.wait_recv()

    place = lax.broadcasted_iota(jnp.int32, (1, cols, 1), 1)
    near = jnp.where(tile == 0, place, cols - 1 - place) < 2
    side = jnp.where(near, field_ref[1].astype(F32), 0.0).astype(BF16)
    ring = jnp.concatenate([field_ref[0], side], axis=1)

    def convolve(cells, taps, bias):
        out_rows = cells.shape[0] - 2
        span = cells.shape[1]
        stacked = jnp.concatenate(
            [cells[r : r + out_rows].reshape(out_rows * span, channels) for r in range(3)], axis=1
        )
        shifted = dot(stacked, taps[...]).reshape(out_rows, span, 3 * channels)
        return (
            pltpu.roll(shifted[:, :, :channels], 1, 1)
            + shifted[:, :, channels : 2 * channels]
            + pltpu.roll(shifted[:, :, 2 * channels :], span - 1, 1)
            + bias
        )

    hidden_map = jnp.maximum(convolve(ring, taps_a, bias_a_ref[...].reshape(1, 1, channels)), 0.0)
    shape = (strip + 2, 2 * cols, 1)
    at_row = lax.broadcasted_iota(jnp.int32, shape, 0) + me * strip - 1
    at_col = lax.broadcasted_iota(jnp.int32, shape, 1)
    in_rows = jnp.logical_and(at_row >= 0, at_row < rows)
    outside = jnp.where(tile == 0, 2 * cols - 1, cols)
    hidden_map = jnp.where(jnp.logical_and(in_rows, at_col != outside), hidden_map, 0.0)
    decoded = convolve(hidden_map.astype(BF16), taps_b, bias_b_ref[...].reshape(1, 1, channels))
    decoded_ref[...] = decoded[:, :cols].astype(BF16)

    peers = depths_ref.at[pl.ds(0, slabs - 1)]
    pltpu.make_async_copy(peers, peers, depth_send).wait()
    peers = parts_ref.at[pl.ds(0, slabs - 1)]
    pltpu.make_async_copy(peers, peers, part_send).wait()
    across.wait_send()

    @pl.when(not_first)
    def _():
        for copy in up:
            copy.wait_send()

    @pl.when(not_last)
    def _():
        for copy in down:
            copy.wait_send()


def body(
    slabs,
    samples,
    counts,
    w_in,
    b_in,
    w_color,
    b_color,
    w_density,
    b_density,
    conv_a,
    bias_a,
    conv_b,
    bias_b,
):
    _, rows, cols, width = samples.shape
    hid, channels = w_color.shape[1:]
    groups = rows * cols // LANES
    strip = rows // slabs
    vmem = pl.BlockSpec(memory_space=pltpu.VMEM)
    smem = pl.BlockSpec(memory_space=pltpu.SMEM)
    hbm = pl.BlockSpec(memory_space=pl.ANY)
    dma = pltpu.SemaphoreType.DMA
    pieces = rows * cols // (2 * LANES)
    decoded, front = pl.pallas_call(
        functools.partial(render_kernel, slabs),
        out_shape=(
            jax.ShapeDtypeStruct((strip, cols, channels), BF16),
            jax.ShapeDtypeStruct((1, cols, rows), F32),
        ),
        in_specs=[hbm] * 7 + [smem] + [hbm] * 4,
        out_specs=(vmem, vmem),
        scratch_shapes=[
            pltpu.VMEM((rows, cols, width), F32),
            pltpu.VMEM((cols, rows), jnp.int32),
            pltpu.VMEM(w_in.shape[1:], F32),
            pltpu.VMEM((1, hid), F32),
            pltpu.VMEM(w_color.shape[1:], F32),
            pltpu.VMEM((1, channels), F32),
            pltpu.VMEM((1, hid), F32),
            pltpu.VMEM(conv_a.shape, BF16),
            pltpu.VMEM((1, channels), F32),
            pltpu.VMEM(conv_b.shape, BF16),
            pltpu.VMEM((1, channels), F32),
            pltpu.VMEM((3 * channels, 3 * channels), BF16),
            pltpu.VMEM((3 * channels, 3 * channels), BF16),
            pltpu.VMEM((K, groups, LANES), F32),
            pltpu.VMEM((groups, K * LANES, channels), BF16),
            pltpu.VMEM((K, groups, LANES), F32),
            pltpu.VMEM((slabs, groups, LANES), F32),
            pltpu.VMEM((slabs, strip * cols, channels), BF16),
            pltpu.VMEM((slabs, strip * cols, channels), BF16),
            pltpu.VMEM((2, strip + 4, cols, channels), BF16),
            dma((10 + pieces,)),
            dma,
            dma,
            dma,
            dma,
            dma((5,)),
            dma((5,)),
        ],
        compiler_params=pltpu.CompilerParams(
            collective_id=0, has_side_effects=True, vmem_limit_bytes=60 * 2**20
        ),
    )(
        samples,
        jnp.swapaxes(counts, 1, 2),
        w_in,
        b_in,
        w_color,
        b_color,
        w_density,
        b_density,
        conv_a,
        bias_a.reshape(1, channels),
        conv_b,
        bias_b.reshape(1, channels),
    )
    return decoded, jnp.swapaxes(front, 1, 2)


def solution(mesh):
    in_specs = (
        P("slab", None, "tile", None),
        P("slab", None, "tile"),
        P("slab", None, None),
        P("slab", None),
        P("slab", None, None),
        P("slab", None),
        P("slab", None),
        P("slab"),
        P(),
        P(),
        P(),
        P(),
    )
    out_specs = (P("slab", "tile", None), P("slab", None, "tile"))
    run = functools.partial(body, mesh.shape["slab"])
    return jax.shard_map(run, mesh=mesh, in_specs=in_specs, out_specs=out_specs, check_vma=False)
```

```python
import functools

import jax
import jax.numpy as jnp
from jax import lax
from jax.experimental import pallas as pl
from jax.experimental.pallas import tpu as pltpu
from jax.sharding import PartitionSpec as P

F = 64
K = 4
LANES = 128
HALVES = 2
MESH = pl.DeviceIdType.MESH
BF16 = jnp.bfloat16
F32 = jnp.float32


def dot(a, b):
    return jnp.dot(a, b, preferred_element_type=F32)


def dot_last(a, b):
    return lax.dot_general(a, b, (((1,), (1,)), ((), ())), preferred_element_type=F32)


def render_kernel(
    slabs,
    samples_hbm,
    counts_hbm,
    w_in_hbm,
    b_in_hbm,
    w_color_hbm,
    b_color_hbm,
    w_density_hbm,
    b_density_ref,
    conv_a_hbm,
    bias_a_hbm,
    conv_b_hbm,
    bias_b_hbm,
    decoded_ref,
    front_ref,
    samples_ref,
    counts_ref,
    w_in_ref,
    b_in_ref,
    w_color_ref,
    b_color_ref,
    w_density_ref,
    conv_a_ref,
    bias_a_ref,
    conv_b_ref,
    bias_b_ref,
    taps_a,
    taps_b,
    density_ref,
    colors_ref,
    weight_ref,
    depths_ref,
    sent_ref,
    parts_ref,
    field_ref,
    load_sems,
    depth_send,
    depth_recv,
    part_send,
    part_recv,
    edge_send,
    edge_recv,
):
    me = lax.axis_index("slab")
    tile = lax.axis_index("tile")
    other = 1 - tile
    rows, cols = samples_ref.shape[0], samples_ref.shape[1]
    groups = rows * cols // LANES
    group_rows = LANES // cols
    strip = rows // slabs
    strip_rays = strip * cols
    hid = w_in_ref.shape[1]
    channels = w_color_ref.shape[1]
    not_first = me > 0
    not_last = me < slabs - 1

    per_half = groups // HALVES
    order = [HALVES * q + h for h in range(HALVES) for q in range(per_half)]
    pieces = [pl.ds(g * group_rows, group_rows) for g in order]
    first_loads = [
        (w_in_hbm.at[0], w_in_ref),
        (b_in_hbm, b_in_ref),
        (w_color_hbm.at[0], w_color_ref),
        (w_density_hbm, w_density_ref),
        (b_color_hbm, b_color_ref),
    ]
    last_loads = [
        (counts_hbm.at[0], counts_ref),
        (conv_a_hbm, conv_a_ref),
        (conv_b_hbm, conv_b_ref),
        (bias_a_hbm, bias_a_ref),
        (bias_b_hbm, bias_b_ref),
    ]
    sample_loads = [(samples_hbm.at[0, piece], samples_ref.at[piece]) for piece in pieces]
    loads = [
        pltpu.make_async_copy(src, dst, load_sems.at[i])
        for i, (src, dst) in enumerate(first_loads + last_loads + sample_loads)
    ]
    sample_loads = loads[len(first_loads) + len(last_loads) :]
    last_loads = loads[len(first_loads) : len(first_loads) + len(last_loads)]
    first_loads = loads[: len(first_loads)]
    for load in first_loads + sample_loads + last_loads:
        load.start()

    barrier = pltpu.get_barrier_semaphore()

    def greet(slab, tile_at):
        pl.semaphore_signal(barrier, inc=1, device_id=(slab, tile_at), device_id_type=MESH)

    def greet_slab(shift, carry):
        greet(lax.rem(me + shift, slabs), tile)
        return carry

    lax.fori_loop(1, slabs, greet_slab, 0)
    greet(me, other)

    @pl.when(not_first)
    def _():
        greet(me - 1, other)

    @pl.when(not_last)
    def _():
        greet(me + 1, other)

    eye = lax.broadcasted_iota(jnp.int32, (LANES, LANES), 0) == lax.broadcasted_iota(
        jnp.int32, (LANES, LANES), 1
    )

    for load in first_loads:
        load.wait()
    w_in = w_in_ref[...]
    high = w_in.astype(BF16)
    low = (w_in - high.astype(F32)).astype(BF16)
    blank = jnp.zeros_like(high)
    even = [high, blank, high, blank, low, blank]
    odd = [blank, high, blank, high, blank, low]
    pair_w = jnp.concatenate(
        [jnp.concatenate(even, axis=0), jnp.concatenate(odd, axis=0)], axis=1
    )
    pair_b = jnp.concatenate([b_in_ref[...], b_in_ref[...]], axis=1)
    density_cols = jnp.transpose(jnp.broadcast_to(w_density_ref[...], (LANES, hid)))
    heads = jnp.concatenate([w_color_ref[...].astype(BF16), density_cols.astype(BF16)], axis=1)
    b_color = b_color_ref[...]
    chunk = 2

    def project(h):
        for c in range(per_half // chunk):
            rays = chunk * LANES
            cells = []
            for q in range(c * chunk, (c + 1) * chunk):
                sample_loads[h * per_half + q].wait()
                start = (HALVES * q + h) * group_rows
                cells.append(samples_ref[start : start + group_rows].reshape(LANES, K * F))
            x = jnp.concatenate(cells, axis=0)
            for pair in range(K // 2):
                part = x[:, pair * LANES : (pair + 1) * LANES]
                part_high = part.astype(BF16)
                part_low = (part - part_high.astype(F32)).astype(BF16)
                both = jnp.concatenate([part_high, part_low, part_high], axis=1)
                act = jnp.maximum(dot(both, pair_w) + pair_b, 0.0).astype(BF16)
                for half in range(2):
                    k = 2 * pair + half
                    out = dot(act[:, half * hid : (half + 1) * hid], heads)
                    color = (out[:, :channels] + b_color).astype(BF16)
                    before = out[:, channels:].reshape(chunk, LANES, LANES)
                    for q in range(chunk):
                        colors_ref[h, c * chunk + q, k * LANES : (k + 1) * LANES, :] = color[
                            q * LANES : (q + 1) * LANES
                        ]
                    density_ref[h, k, c * chunk : (c + 1) * chunk, :] = jnp.sum(
                        jnp.where(eye, before, 0.0), axis=1
                    )

    def send_depth(h):
        density = []
        for k in range(K):
            z = density_ref[h, k] + b_density_ref[0]
            soft = jnp.maximum(z, 0.0) + jnp.log1p(jnp.exp(-jnp.abs(z)))
            density.append(jnp.where(live[h] > k, soft, 0.0))
        depths_ref[h, me] = density[0] + density[1] + density[2] + density[3]
        if h == 0:
            pl.semaphore_wait(
                barrier, slabs + not_first.astype(jnp.int32) + not_last.astype(jnp.int32)
            )

        def send(shift, carry):
            pltpu.make_async_remote_copy(
                src_ref=depths_ref.at[h, me],
                dst_ref=depths_ref.at[h, me],
                send_sem=depth_send.at[h],
                recv_sem=depth_recv.at[h],
                device_id=(lax.rem(me + shift, slabs), tile),
                device_id_type=MESH,
            ).start()
            return carry

        lax.fori_loop(1, slabs, send, 0)
        return density

    def weigh(h, density):
        peers = depths_ref.at[h, pl.ds(0, slabs - 1)]
        pltpu.make_async_copy(peers, peers, depth_recv.at[h]).wait()
        total = depths_ref[h, 0]
        prefix = jnp.where(me > 0, total, 0.0)
        for s in range(1, slabs):
            one = depths_ref[h, s]
            total = total + one
            prefix = prefix + jnp.where(s < me, one, 0.0)
        front = prefix / total
        ahead = front
        for k in range(K):
            scaled = density[k] / total
            weight_ref[h, k] = jnp.exp(-ahead) * (1.0 - jnp.exp(-scaled))
            ahead = ahead + scaled
        return front

    def send_part(owner):
        pltpu.make_async_remote_copy(
            src_ref=sent_ref.at[owner],
            dst_ref=parts_ref.at[me],
            send_sem=part_send,
            recv_sem=part_recv,
            device_id=(owner, tile),
            device_id_type=MESH,
        ).start()

    strips = LANES // strip_rays

    def scatter(h):
        for i in range(per_half):
            q = lax.rem(me // (strips * HALVES) + i, per_half)
            diag = [
                jnp.where(eye, weight_ref[h, k, pl.ds(q, 1), :], 0.0).astype(BF16)
                for k in range(K)
            ]
            image = dot(jnp.concatenate(diag, axis=1), colors_ref[h, q]).astype(BF16)
            first = strips * (HALVES * q + h)
            sent_ref[pl.ds(first, strips)] = image.reshape(strips, strip_rays, channels)
            for j in range(strips):
                owner = first + j
                if i > 0:
                    send_part(owner)
                else:
                    pl.when(owner != me)(functools.partial(send_part, owner))

    project(0)

    for load in last_loads:
        load.wait()
    spread = (
        lax.rem(lax.broadcasted_iota(jnp.int32, (cols, LANES), 1), cols)
        == lax.broadcasted_iota(jnp.int32, (cols, LANES), 0)
    ).astype(BF16)
    own_lane = (
        lax.broadcasted_iota(jnp.int32, (group_rows, LANES), 1) // cols
        == lax.broadcasted_iota(jnp.int32, (group_rows, LANES), 0)
    )
    row_eye = (
        lax.broadcasted_iota(jnp.int32, (rows, rows), 0)
        == lax.broadcasted_iota(jnp.int32, (rows, rows), 1)
    ).astype(BF16)
    by_row = dot_last(row_eye, counts_ref[...].astype(F32).astype(BF16)).astype(BF16)
    spread_counts = dot(by_row, spread).reshape(per_half, HALVES, group_rows, LANES)
    live = [
        jnp.sum(jnp.where(own_lane, spread_counts[:, h], 0.0), axis=1) for h in range(HALVES)
    ]

    densities = [send_depth(0)]
    for h in range(1, HALVES):
        project(h)
        densities.append(send_depth(h))
    fronts = []
    for h in range(HALVES):
        fronts.append(weigh(h, densities[h]))
        scatter(h)
    parts_ref[me] = sent_ref[me]

    for taps, conv in ((taps_a, conv_a_ref), (taps_b, conv_b_ref)):
        for r in range(3):
            for s in range(3):
                taps[r * channels : (r + 1) * channels, s * channels : (s + 1) * channels] = conv[
                    r, s
                ]

    laid = jnp.stack(
        [jnp.where(own_lane, front[:, None, :], 0.0) for front in fronts], axis=1
    ).reshape(rows, LANES)
    first = laid.astype(BF16)
    rest = laid - first.astype(F32)
    second = rest.astype(BF16)
    third = (rest - second.astype(F32)).astype(BF16)
    front_ref[0] = dot_last(spread, first) + dot_last(spread, second) + dot_last(spread, third)

    peers = parts_ref.at[pl.ds(0, slabs - 1)]
    pltpu.make_async_copy(peers, peers, part_recv).wait()
    image = parts_ref[0].astype(F32)
    for s in range(1, slabs):
        image = image + parts_ref[s].astype(F32)
    image = image.astype(BF16).reshape(strip, cols, channels)

    field_ref[0, 2 : 2 + strip] = image
    edge = jnp.zeros((2, 2, cols, channels), BF16)

    def edge_copy(which, source, target, device):
        return pltpu.make_async_remote_copy(
            src_ref=source,
            dst_ref=target,
            send_sem=edge_send.at[which],
            recv_sem=edge_recv.at[which],
            device_id=device,
            device_id_type=MESH,
        )

    own = field_ref.at[0, pl.ds(2, strip)]
    head = field_ref.at[0, pl.ds(2, 2)]
    tail = field_ref.at[0, pl.ds(strip, 2)]
    up = [
        edge_copy(1, head, field_ref.at[0, pl.ds(strip + 2, 2)], (me - 1, tile)),
        edge_copy(2, head, field_ref.at[1, pl.ds(strip + 2, 2)], (me - 1, other)),
    ]
    down = [
        edge_copy(3, tail, field_ref.at[0, pl.ds(0, 2)], (me + 1, tile)),
        edge_copy(4, tail, field_ref.at[1, pl.ds(0, 2)], (me + 1, other)),
    ]
    across = edge_copy(0, own, field_ref.at[1, pl.ds(2, strip)], (me, other))

    @pl.when(not_first)
    def _():
        for copy in up:
            copy.start()

    @pl.when(not_last)
    def _():
        for copy in down:
            copy.start()

    across.start()

    @pl.when(jnp.logical_not(not_first))
    def _():
        field_ref[:, 0:2] = edge

    @pl.when(jnp.logical_not(not_last))
    def _():
        field_ref[:, strip + 2 : strip + 4] = edge

    @pl.when(not_last)
    def _():
        for copy in up:
            copy.wait_recv()

    @pl.when(not_first)
    def _():
        for copy in down:
            copy.wait_recv()

    across.wait_recv()

    place = lax.broadcasted_iota(jnp.int32, (1, cols, 1), 1)
    near = jnp.where(tile == 0, place, cols - 1 - place) < 2
    side = jnp.where(near, field_ref[1].astype(F32), 0.0).astype(BF16)
    ring = jnp.concatenate([field_ref[0], side], axis=1)

    def convolve(cells, taps, bias):
        out_rows = cells.shape[0] - 2
        span = cells.shape[1]
        stacked = jnp.concatenate(
            [cells[r : r + out_rows].reshape(out_rows * span, channels) for r in range(3)], axis=1
        )
        shifted = dot(stacked, taps[...]).reshape(out_rows, span, 3 * channels)
        return (
            pltpu.roll(shifted[:, :, :channels], 1, 1)
            + shifted[:, :, channels : 2 * channels]
            + pltpu.roll(shifted[:, :, 2 * channels :], span - 1, 1)
            + bias
        )

    hidden_map = jnp.maximum(convolve(ring, taps_a, bias_a_ref[...].reshape(1, 1, channels)), 0.0)
    shape = (strip + 2, 2 * cols, 1)
    at_row = lax.broadcasted_iota(jnp.int32, shape, 0) + me * strip - 1
    at_col = lax.broadcasted_iota(jnp.int32, shape, 1)
    in_rows = jnp.logical_and(at_row >= 0, at_row < rows)
    outside = jnp.where(tile == 0, 2 * cols - 1, cols)
    hidden_map = jnp.where(jnp.logical_and(in_rows, at_col != outside), hidden_map, 0.0)
    decoded = convolve(hidden_map.astype(BF16), taps_b, bias_b_ref[...].reshape(1, 1, channels))
    decoded_ref[...] = decoded[:, :cols].astype(BF16)

    for h in range(HALVES):
        peers = depths_ref.at[h, pl.ds(0, slabs - 1)]
        pltpu.make_async_copy(peers, peers, depth_send.at[h]).wait()
    peers = parts_ref.at[pl.ds(0, slabs - 1)]
    pltpu.make_async_copy(peers, peers, part_send).wait()
    across.wait_send()

    @pl.when(not_first)
    def _():
        for copy in up:
            copy.wait_send()

    @pl.when(not_last)
    def _():
        for copy in down:
            copy.wait_send()


def body(
    slabs,
    samples,
    counts,
    w_in,
    b_in,
    w_color,
    b_color,
    w_density,
    b_density,
    conv_a,
    bias_a,
    conv_b,
    bias_b,
):
    _, rows, cols, width = samples.shape
    hid, channels = w_color.shape[1:]
    groups = rows * cols // LANES
    strip = rows // slabs
    vmem = pl.BlockSpec(memory_space=pltpu.VMEM)
    smem = pl.BlockSpec(memory_space=pltpu.SMEM)
    hbm = pl.BlockSpec(memory_space=pl.ANY)
    dma = pltpu.SemaphoreType.DMA
    per_half = groups // HALVES
    decoded, front = pl.pallas_call(
        functools.partial(render_kernel, slabs),
        out_shape=(
            jax.ShapeDtypeStruct((strip, cols, channels), BF16),
            jax.ShapeDtypeStruct((1, cols, rows), F32),
        ),
        in_specs=[hbm] * 7 + [smem] + [hbm] * 4,
        out_specs=(vmem, vmem),
        scratch_shapes=[
            pltpu.VMEM((rows, cols, width), F32),
            pltpu.VMEM((cols, rows), jnp.int32),
            pltpu.VMEM(w_in.shape[1:], F32),
            pltpu.VMEM((1, hid), F32),
            pltpu.VMEM(w_color.shape[1:], F32),
            pltpu.VMEM((1, channels), F32),
            pltpu.VMEM((1, hid), F32),
            pltpu.VMEM(conv_a.shape, BF16),
            pltpu.VMEM((1, channels), F32),
            pltpu.VMEM(conv_b.shape, BF16),
            pltpu.VMEM((1, channels), F32),
            pltpu.VMEM((3 * channels, 3 * channels), BF16),
            pltpu.VMEM((3 * channels, 3 * channels), BF16),
            pltpu.VMEM((HALVES, K, per_half, LANES), F32),
            pltpu.VMEM((HALVES, per_half, K * LANES, channels), BF16),
            pltpu.VMEM((HALVES, K, per_half, LANES), F32),
            pltpu.VMEM((HALVES, slabs, per_half, LANES), F32),
            pltpu.VMEM((slabs, strip * cols, channels), BF16),
            pltpu.VMEM((slabs, strip * cols, channels), BF16),
            pltpu.VMEM((2, strip + 4, cols, channels), BF16),
            dma((10 + groups,)),
            dma((HALVES,)),
            dma((HALVES,)),
            dma,
            dma,
            dma((5,)),
            dma((5,)),
        ],
        compiler_params=pltpu.CompilerParams(
            collective_id=0, has_side_effects=True, vmem_limit_bytes=60 * 2**20
        ),
    )(
        samples,
        jnp.swapaxes(counts, 1, 2),
        w_in,
        b_in,
        w_color,
        b_color,
        w_density,
        b_density,
        conv_a,
        bias_a.reshape(1, channels),
        conv_b,
        bias_b.reshape(1, channels),
    )
    return decoded, jnp.swapaxes(front, 1, 2)


def solution(mesh):
    in_specs = (
        P("slab", None, "tile", None),
        P("slab", None, "tile"),
        P("slab", None, None),
        P("slab", None),
        P("slab", None, None),
        P("slab", None),
        P("slab", None),
        P("slab"),
        P(),
        P(),
        P(),
        P(),
    )
    out_specs = (P("slab", "tile", None), P("slab", None, "tile"))
    run = functools.partial(body, mesh.shape["slab"])
    return jax.shard_map(run, mesh=mesh, in_specs=in_specs, out_specs=out_specs, check_vma=False)
```

```python
import functools

import jax
import jax.numpy as jnp
from jax import lax
from jax.experimental import pallas as pl
from jax.experimental.pallas import tpu as pltpu
from jax.sharding import PartitionSpec as P

F = 64
K = 4
LANES = 128
HALVES = 2
PLANES = 4
MESH = pl.DeviceIdType.MESH
BF16 = jnp.bfloat16
F32 = jnp.float32


def dot(a, b):
    return jnp.dot(a, b, preferred_element_type=F32)


def dot_last(a, b):
    return lax.dot_general(a, b, (((1,), (1,)), ((), ())), preferred_element_type=F32)


def render_kernel(
    slabs,
    samples_hbm,
    counts_hbm,
    w_in_hbm,
    b_in_hbm,
    w_color_hbm,
    b_color_hbm,
    w_density_hbm,
    b_density_hbm,
    conv_a_hbm,
    bias_a_hbm,
    conv_b_hbm,
    bias_b_hbm,
    decoded_ref,
    front_ref,
    samples_ref,
    counts_ref,
    w_in_ref,
    b_in_ref,
    w_color_ref,
    b_color_ref,
    w_density_ref,
    b_density_ref,
    conv_a_ref,
    bias_a_ref,
    conv_b_ref,
    bias_b_ref,
    taps_a,
    taps_b,
    density_ref,
    colors_ref,
    weight_ref,
    depths_ref,
    sent_ref,
    parts_ref,
    held_ref,
    sums_ref,
    field_ref,
    load_sems,
    depth_send,
    depth_recv,
    part_send,
    part_recv,
    sum_send,
    sum_recv,
    edge_send,
    edge_recv,
):
    me = lax.axis_index("slab")
    tile = lax.axis_index("tile")
    other = 1 - tile
    rows, cols = samples_ref.shape[0], samples_ref.shape[1]
    groups = rows * cols // LANES
    group_rows = LANES // cols
    strip = rows // slabs
    strip_rays = strip * cols
    hid = w_in_ref.shape[1]
    channels = w_color_ref.shape[1]
    not_first = me > 0
    not_last = me < slabs - 1

    plane = slabs // PLANES
    my_plane, my_spot = me // plane, lax.rem(me, plane)
    strips = LANES // strip_rays
    plane_groups = plane // strips
    folds = PLANES // HALVES
    per_half = groups // HALVES
    order = [
        (HALVES * fold + h) * plane_groups + r
        for h in range(HALVES)
        for fold in range(folds)
        for r in range(plane_groups)
    ]
    pieces = [pl.ds(g * group_rows, group_rows) for g in order]
    first_loads = [
        (w_in_hbm.at[0], w_in_ref),
        (b_in_hbm, b_in_ref),
        (w_color_hbm.at[0], w_color_ref),
        (w_density_hbm, w_density_ref),
        (b_color_hbm, b_color_ref),
    ]
    last_loads = [
        (counts_hbm.at[0], counts_ref),
        (conv_a_hbm, conv_a_ref),
        (conv_b_hbm, conv_b_ref),
        (b_density_hbm, b_density_ref),
        (bias_a_hbm, bias_a_ref),
        (bias_b_hbm, bias_b_ref),
    ]
    sample_loads = [(samples_hbm.at[0, piece], samples_ref.at[piece]) for piece in pieces]
    loads = [
        pltpu.make_async_copy(src, dst, load_sems.at[i])
        for i, (src, dst) in enumerate(first_loads + last_loads + sample_loads)
    ]
    sample_loads = loads[len(first_loads) + len(last_loads) :]
    last_loads = loads[len(first_loads) : len(first_loads) + len(last_loads)]
    first_loads = loads[: len(first_loads)]
    for load in first_loads + sample_loads + last_loads:
        load.start()

    barrier = pltpu.get_barrier_semaphore()

    def greet(slab, tile_at):
        pl.semaphore_signal(barrier, inc=1, device_id=(slab, tile_at), device_id_type=MESH)

    def greet_slab(shift, carry):
        greet(lax.rem(me + shift, slabs), tile)
        return carry

    lax.fori_loop(1, slabs, greet_slab, 0)
    greet(me, other)

    @pl.when(not_first)
    def _():
        greet(me - 1, other)

    @pl.when(not_last)
    def _():
        greet(me + 1, other)

    eye = lax.broadcasted_iota(jnp.int32, (LANES, LANES), 0) == lax.broadcasted_iota(
        jnp.int32, (LANES, LANES), 1
    )

    for load in first_loads:
        load.wait()
    w_in = w_in_ref[...]
    high = w_in.astype(BF16)
    low = (w_in - high.astype(F32)).astype(BF16)
    blank = jnp.zeros_like(high)
    even = [high, blank, high, blank, low, blank]
    odd = [blank, high, blank, high, blank, low]
    pair_w = jnp.concatenate(
        [jnp.concatenate(even, axis=0), jnp.concatenate(odd, axis=0)], axis=1
    )
    pair_b = jnp.concatenate([b_in_ref[...], b_in_ref[...]], axis=1)
    density_cols = jnp.transpose(jnp.broadcast_to(w_density_ref[...], (LANES, hid)))
    heads = jnp.concatenate([w_color_ref[...].astype(BF16), density_cols.astype(BF16)], axis=1)
    b_color = b_color_ref[...]
    chunk = 2

    def project(h):
        for c in range(per_half // chunk):
            rays = chunk * LANES
            cells = []
            for q in range(c * chunk, (c + 1) * chunk):
                sample_loads[h * per_half + q].wait()
                start = order[h * per_half + q] * group_rows
                cells.append(samples_ref[start : start + group_rows].reshape(LANES, K * F))
            x = jnp.concatenate(cells, axis=0)
            for pair in range(K // 2):
                part = x[:, pair * LANES : (pair + 1) * LANES]
                part_high = part.astype(BF16)
                part_low = (part - part_high.astype(F32)).astype(BF16)
                both = jnp.concatenate([part_high, part_low, part_high], axis=1)
                act = jnp.maximum(dot(both, pair_w) + pair_b, 0.0).astype(BF16)
                for half in range(2):
                    k = 2 * pair + half
                    out = dot(act[:, half * hid : (half + 1) * hid], heads)
                    color = (out[:, :channels] + b_color).astype(BF16)
                    before = out[:, channels:].reshape(chunk, LANES, LANES)
                    for q in range(chunk):
                        colors_ref[h, c * chunk + q, k * LANES : (k + 1) * LANES, :] = color[
                            q * LANES : (q + 1) * LANES
                        ]
                    density_ref[h, k, c * chunk : (c + 1) * chunk, :] = jnp.sum(
                        jnp.where(eye, before, 0.0), axis=1
                    )

    def send_depth(h):
        density = []
        for k in range(K):
            z = density_ref[h, k] + b_density_ref[0]
            soft = jnp.maximum(z, 0.0) + jnp.log1p(jnp.exp(-jnp.abs(z)))
            density.append(jnp.where(live[h] > k, soft, 0.0))
        depths_ref[h, me] = density[0] + density[1] + density[2] + density[3]
        if h == 0:
            pl.semaphore_wait(
                barrier, slabs + not_first.astype(jnp.int32) + not_last.astype(jnp.int32)
            )

        def send(shift, carry):
            pltpu.make_async_remote_copy(
                src_ref=depths_ref.at[h, me],
                dst_ref=depths_ref.at[h, me],
                send_sem=depth_send.at[h],
                recv_sem=depth_recv.at[h],
                device_id=(lax.rem(me + shift, slabs), tile),
                device_id_type=MESH,
            ).start()
            return carry

        lax.fori_loop(1, slabs, send, 0)
        return density

    def weigh(h, density):
        peers = depths_ref.at[h, pl.ds(0, slabs - 1)]
        pltpu.make_async_copy(peers, peers, depth_recv.at[h]).wait()
        total = depths_ref[h, 0]
        prefix = jnp.where(me > 0, total, 0.0)
        for s in range(1, slabs):
            one = depths_ref[h, s]
            total = total + one
            prefix = prefix + jnp.where(s < me, one, 0.0)
        front = prefix / total
        ahead = front
        for k in range(K):
            scaled = density[k] / total
            weight_ref[h, k] = jnp.exp(-ahead) * (1.0 - jnp.exp(-scaled))
            ahead = ahead + scaled
        return front

    def send_part(h, spot):
        pltpu.make_async_remote_copy(
            src_ref=sent_ref.at[h, spot],
            dst_ref=parts_ref.at[h, my_spot],
            send_sem=part_send.at[h],
            recv_sem=part_recv.at[h],
            device_id=(my_plane * plane + spot, tile),
            device_id_type=MESH,
        ).start()

    def scatter(h):
        for i in range(1, plane_groups + 1):
            r = lax.rem(my_spot // strips + i, plane_groups)
            for fold in range(folds):
                q = fold * plane_groups + r
                diag = [
                    jnp.where(eye, weight_ref[h, k, pl.ds(q, 1), :], 0.0).astype(BF16)
                    for k in range(K)
                ]
                image = dot(jnp.concatenate(diag, axis=1), colors_ref[h, q]).astype(BF16)
                image = image.reshape(strips, strip_rays, channels)
                for j in range(strips):
                    sent_ref[h, strips * r + j, fold] = image[j]
            for j in range(strips):
                spot = strips * r + j
                if i < plane_groups:
                    send_part(h, spot)
                else:
                    pl.when(spot != my_spot)(functools.partial(send_part, h, spot))
        parts_ref[h, my_spot] = sent_ref[h, my_spot]

    def forward(h):
        peers = parts_ref.at[h, pl.ds(0, plane - 1)]
        pltpu.make_async_copy(peers, peers, part_recv.at[h]).wait()
        for fold in range(folds):
            part = parts_ref[h, 0, fold].astype(F32)
            for s in range(1, plane):
                part = part + parts_ref[h, s, fold].astype(F32)
            held_ref[h, fold] = part.astype(BF16)
            owner = HALVES * fold + h

            def keep(fold=fold):
                sums_ref[my_plane] = held_ref[h, fold]

            def send(fold=fold, owner=owner):
                pltpu.make_async_remote_copy(
                    src_ref=held_ref.at[h, fold],
                    dst_ref=sums_ref.at[my_plane],
                    send_sem=sum_send,
                    recv_sem=sum_recv,
                    device_id=(owner * plane + my_spot, tile),
                    device_id_type=MESH,
                ).start()

            pl.when(owner != my_plane)(send)
            pl.when(owner == my_plane)(keep)

    project(0)

    for load in last_loads:
        load.wait()
    spread = (
        lax.rem(lax.broadcasted_iota(jnp.int32, (cols, LANES), 1), cols)
        == lax.broadcasted_iota(jnp.int32, (cols, LANES), 0)
    ).astype(BF16)
    own_lane = (
        lax.broadcasted_iota(jnp.int32, (group_rows, LANES), 1) // cols
        == lax.broadcasted_iota(jnp.int32, (group_rows, LANES), 0)
    )
    row_eye = (
        lax.broadcasted_iota(jnp.int32, (rows, rows), 0)
        == lax.broadcasted_iota(jnp.int32, (rows, rows), 1)
    ).astype(BF16)
    by_row = dot_last(row_eye, counts_ref[...].astype(F32).astype(BF16)).astype(BF16)
    spread_counts = dot(by_row, spread).reshape(folds, HALVES, plane_groups, group_rows, LANES)
    live = [
        jnp.sum(
            jnp.where(own_lane, spread_counts[:, h].reshape(per_half, group_rows, LANES), 0.0),
            axis=1,
        )
        for h in range(HALVES)
    ]

    densities = [send_depth(0)]
    for h in range(1, HALVES):
        project(h)
        densities.append(send_depth(h))
    fronts = []
    for h in range(HALVES):
        fronts.append(weigh(h, densities[h]))
        scatter(h)
    for h in range(HALVES):
        forward(h)

    for taps, conv in ((taps_a, conv_a_ref), (taps_b, conv_b_ref)):
        for r in range(3):
            for s in range(3):
                taps[r * channels : (r + 1) * channels, s * channels : (s + 1) * channels] = conv[
                    r, s
                ]

    laid = jnp.stack(
        [
            jnp.where(own_lane, front[:, None, :], 0.0).reshape(
                folds, plane_groups, group_rows, LANES
            )
            for front in fronts
        ],
        axis=1,
    ).reshape(rows, LANES)
    first = laid.astype(BF16)
    rest = laid - first.astype(F32)
    second = rest.astype(BF16)
    third = (rest - second.astype(F32)).astype(BF16)
    front_ref[0] = dot_last(spread, first) + dot_last(spread, second) + dot_last(spread, third)

    peers = sums_ref.at[pl.ds(0, PLANES - 1)]
    pltpu.make_async_copy(peers, peers, sum_recv).wait()
    image = sums_ref[0].astype(F32)
    for s in range(1, PLANES):
        image = image + sums_ref[s].astype(F32)
    image = image.astype(BF16).reshape(strip, cols, channels)

    field_ref[0, 2 : 2 + strip] = image
    edge = jnp.zeros((2, 2, cols, channels), BF16)

    def edge_copy(which, source, target, device):
        return pltpu.make_async_remote_copy(
            src_ref=source,
            dst_ref=target,
            send_sem=edge_send.at[which],
            recv_sem=edge_recv.at[which],
            device_id=device,
            device_id_type=MESH,
        )

    own = field_ref.at[0, pl.ds(2, strip)]
    head = field_ref.at[0, pl.ds(2, 2)]
    tail = field_ref.at[0, pl.ds(strip, 2)]
    up = [
        edge_copy(1, head, field_ref.at[0, pl.ds(strip + 2, 2)], (me - 1, tile)),
        edge_copy(2, head, field_ref.at[1, pl.ds(strip + 2, 2)], (me - 1, other)),
    ]
    down = [
        edge_copy(3, tail, field_ref.at[0, pl.ds(0, 2)], (me + 1, tile)),
        edge_copy(4, tail, field_ref.at[1, pl.ds(0, 2)], (me + 1, other)),
    ]
    across = edge_copy(0, own, field_ref.at[1, pl.ds(2, strip)], (me, other))

    @pl.when(not_first)
    def _():
        for copy in up:
            copy.start()

    @pl.when(not_last)
    def _():
        for copy in down:
            copy.start()

    across.start()

    @pl.when(jnp.logical_not(not_first))
    def _():
        field_ref[:, 0:2] = edge

    @pl.when(jnp.logical_not(not_last))
    def _():
        field_ref[:, strip + 2 : strip + 4] = edge

    @pl.when(not_last)
    def _():
        for copy in up:
            copy.wait_recv()

    @pl.when(not_first)
    def _():
        for copy in down:
            copy.wait_recv()

    across.wait_recv()

    place = lax.broadcasted_iota(jnp.int32, (1, cols, 1), 1)
    near = jnp.where(tile == 0, place, cols - 1 - place) < 2
    side = jnp.where(near, field_ref[1].astype(F32), 0.0).astype(BF16)
    ring = jnp.concatenate([field_ref[0], side], axis=1)

    def convolve(cells, taps, bias):
        out_rows = cells.shape[0] - 2
        span = cells.shape[1]
        stacked = jnp.concatenate(
            [cells[r : r + out_rows].reshape(out_rows * span, channels) for r in range(3)], axis=1
        )
        shifted = dot(stacked, taps[...]).reshape(out_rows, span, 3 * channels)
        return (
            pltpu.roll(shifted[:, :, :channels], 1, 1)
            + shifted[:, :, channels : 2 * channels]
            + pltpu.roll(shifted[:, :, 2 * channels :], span - 1, 1)
            + bias
        )

    hidden_map = jnp.maximum(convolve(ring, taps_a, bias_a_ref[...].reshape(1, 1, channels)), 0.0)
    shape = (strip + 2, 2 * cols, 1)
    at_row = lax.broadcasted_iota(jnp.int32, shape, 0) + me * strip - 1
    at_col = lax.broadcasted_iota(jnp.int32, shape, 1)
    in_rows = jnp.logical_and(at_row >= 0, at_row < rows)
    outside = jnp.where(tile == 0, 2 * cols - 1, cols)
    hidden_map = jnp.where(jnp.logical_and(in_rows, at_col != outside), hidden_map, 0.0)
    decoded = convolve(hidden_map.astype(BF16), taps_b, bias_b_ref[...].reshape(1, 1, channels))
    decoded_ref[...] = decoded[:, :cols].astype(BF16)

    for h in range(HALVES):
        peers = depths_ref.at[h, pl.ds(0, slabs - 1)]
        pltpu.make_async_copy(peers, peers, depth_send.at[h]).wait()
        peers = parts_ref.at[h, pl.ds(0, plane - 1)]
        pltpu.make_async_copy(peers, peers, part_send.at[h]).wait()
    pltpu.make_async_copy(
        sums_ref.at[pl.ds(0, PLANES - 1)], sums_ref.at[pl.ds(0, PLANES - 1)], sum_send
    ).wait()
    across.wait_send()

    @pl.when(not_first)
    def _():
        for copy in up:
            copy.wait_send()

    @pl.when(not_last)
    def _():
        for copy in down:
            copy.wait_send()


def body(
    slabs,
    samples,
    counts,
    w_in,
    b_in,
    w_color,
    b_color,
    w_density,
    b_density,
    conv_a,
    bias_a,
    conv_b,
    bias_b,
):
    _, rows, cols, width = samples.shape
    hid, channels = w_color.shape[1:]
    groups = rows * cols // LANES
    strip = rows // slabs
    vmem = pl.BlockSpec(memory_space=pltpu.VMEM)
    hbm = pl.BlockSpec(memory_space=pl.ANY)
    dma = pltpu.SemaphoreType.DMA
    per_half = groups // HALVES
    decoded, front = pl.pallas_call(
        functools.partial(render_kernel, slabs),
        out_shape=(
            jax.ShapeDtypeStruct((strip, cols, channels), BF16),
            jax.ShapeDtypeStruct((1, cols, rows), F32),
        ),
        in_specs=[hbm] * 12,
        out_specs=(vmem, vmem),
        scratch_shapes=[
            pltpu.VMEM((rows, cols, width), F32),
            pltpu.VMEM((cols, rows), jnp.int32),
            pltpu.VMEM(w_in.shape[1:], F32),
            pltpu.VMEM((1, hid), F32),
            pltpu.VMEM(w_color.shape[1:], F32),
            pltpu.VMEM((1, channels), F32),
            pltpu.VMEM((1, hid), F32),
            pltpu.SMEM((1,), F32),
            pltpu.VMEM(conv_a.shape, BF16),
            pltpu.VMEM((1, channels), F32),
            pltpu.VMEM(conv_b.shape, BF16),
            pltpu.VMEM((1, channels), F32),
            pltpu.VMEM((3 * channels, 3 * channels), BF16),
            pltpu.VMEM((3 * channels, 3 * channels), BF16),
            pltpu.VMEM((HALVES, K, per_half, LANES), F32),
            pltpu.VMEM((HALVES, per_half, K * LANES, channels), BF16),
            pltpu.VMEM((HALVES, K, per_half, LANES), F32),
            pltpu.VMEM((HALVES, slabs, per_half, LANES), F32),
            pltpu.VMEM((HALVES, slabs // PLANES, PLANES // HALVES, strip * cols, channels), BF16),
            pltpu.VMEM((HALVES, slabs // PLANES, PLANES // HALVES, strip * cols, channels), BF16),
            pltpu.VMEM((HALVES, PLANES // HALVES, strip * cols, channels), BF16),
            pltpu.VMEM((PLANES, strip * cols, channels), BF16),
            pltpu.VMEM((2, strip + 4, cols, channels), BF16),
            dma((11 + groups,)),
            dma((HALVES,)),
            dma((HALVES,)),
            dma((HALVES,)),
            dma((HALVES,)),
            dma,
            dma,
            dma((5,)),
            dma((5,)),
        ],
        compiler_params=pltpu.CompilerParams(
            collective_id=0, has_side_effects=True, vmem_limit_bytes=60 * 2**20
        ),
    )(
        samples,
        jnp.swapaxes(counts, 1, 2),
        w_in,
        b_in,
        w_color,
        b_color,
        w_density,
        b_density,
        conv_a,
        bias_a.reshape(1, channels),
        conv_b,
        bias_b.reshape(1, channels),
    )
    return decoded, jnp.swapaxes(front, 1, 2)


def solution(mesh):
    in_specs = (
        P("slab", None, "tile", None),
        P("slab", None, "tile"),
        P("slab", None, None),
        P("slab", None),
        P("slab", None, None),
        P("slab", None),
        P("slab", None),
        P("slab"),
        P(),
        P(),
        P(),
        P(),
    )
    out_specs = (P("slab", "tile", None), P("slab", None, "tile"))
    run = functools.partial(body, mesh.shape["slab"])
    return jax.shard_map(run, mesh=mesh, in_specs=in_specs, out_specs=out_specs, check_vma=False)
```

```python
import functools

import jax
import jax.numpy as jnp
from jax import lax
from jax.experimental import pallas as pl
from jax.experimental.pallas import tpu as pltpu
from jax.sharding import PartitionSpec as P

F = 64
K = 4
LANES = 128
HALVES = 2
MESH = pl.DeviceIdType.MESH
BF16 = jnp.bfloat16
F32 = jnp.float32


def dot(a, b):
    return jnp.dot(a, b, preferred_element_type=F32)


def dot_last(a, b):
    return lax.dot_general(a, b, (((1,), (1,)), ((), ())), preferred_element_type=F32)


def render_kernel(
    slabs,
    samples_hbm,
    counts_hbm,
    w_in_hbm,
    b_in_hbm,
    w_color_hbm,
    b_color_hbm,
    w_density_hbm,
    b_density_ref,
    conv_a_hbm,
    bias_a_hbm,
    conv_b_hbm,
    bias_b_hbm,
    decoded_ref,
    front_ref,
    samples_ref,
    counts_ref,
    w_in_ref,
    b_in_ref,
    w_color_ref,
    b_color_ref,
    w_density_ref,
    conv_a_ref,
    bias_a_ref,
    conv_b_ref,
    bias_b_ref,
    taps_a,
    taps_b,
    density_ref,
    colors_ref,
    weight_ref,
    depths_ref,
    sent_ref,
    parts_ref,
    field_ref,
    load_sems,
    depth_send,
    depth_recv,
    part_send,
    part_recv,
    edge_send,
    edge_recv,
):
    me = lax.axis_index("slab")
    tile = lax.axis_index("tile")
    other = 1 - tile
    rows, cols = samples_ref.shape[0], samples_ref.shape[1]
    groups = rows * cols // LANES
    group_rows = LANES // cols
    strip = rows // slabs
    strip_rays = strip * cols
    hid = w_in_ref.shape[1]
    channels = w_color_ref.shape[1]
    not_first = me > 0
    not_last = me < slabs - 1

    per_half = groups // HALVES
    order = [HALVES * q + h for h in range(HALVES) for q in range(per_half)]
    pieces = [pl.ds(g * group_rows, group_rows) for g in order]
    first_loads = [
        (w_in_hbm.at[0], w_in_ref),
        (b_in_hbm, b_in_ref),
        (w_color_hbm.at[0], w_color_ref),
        (w_density_hbm, w_density_ref),
        (b_color_hbm, b_color_ref),
    ]
    last_loads = [
        (counts_hbm.at[0], counts_ref),
        (conv_a_hbm, conv_a_ref),
        (conv_b_hbm, conv_b_ref),
        (bias_a_hbm, bias_a_ref),
        (bias_b_hbm, bias_b_ref),
    ]
    sample_loads = [(samples_hbm.at[0, piece], samples_ref.at[piece]) for piece in pieces]
    loads = [
        pltpu.make_async_copy(src, dst, load_sems.at[i])
        for i, (src, dst) in enumerate(first_loads + last_loads + sample_loads)
    ]
    sample_loads = loads[len(first_loads) + len(last_loads) :]
    last_loads = loads[len(first_loads) : len(first_loads) + len(last_loads)]
    first_loads = loads[: len(first_loads)]
    for load in first_loads + sample_loads + last_loads:
        load.start()

    barrier = pltpu.get_barrier_semaphore()

    def greet(slab, tile_at):
        pl.semaphore_signal(barrier, inc=1, device_id=(slab, tile_at), device_id_type=MESH)

    def greet_slab(shift, carry):
        greet(lax.rem(me + shift, slabs), tile)
        return carry

    lax.fori_loop(1, slabs, greet_slab, 0)
    greet(me, other)

    @pl.when(not_first)
    def _():
        greet(me - 1, other)

    @pl.when(not_last)
    def _():
        greet(me + 1, other)

    eye = lax.broadcasted_iota(jnp.int32, (LANES, LANES), 0) == lax.broadcasted_iota(
        jnp.int32, (LANES, LANES), 1
    )

    for load in first_loads:
        load.wait()
    w_in = w_in_ref[...].astype(BF16)
    blank = jnp.zeros_like(w_in)
    pair_w = jnp.concatenate(
        [jnp.concatenate([w_in, blank], axis=0), jnp.concatenate([blank, w_in], axis=0)], axis=1
    )
    pair_b = jnp.concatenate([b_in_ref[...], b_in_ref[...]], axis=1)
    density_cols = jnp.transpose(jnp.broadcast_to(w_density_ref[...], (LANES, hid)))
    heads = jnp.concatenate([w_color_ref[...].astype(BF16), density_cols.astype(BF16)], axis=1)
    b_color = b_color_ref[...]
    chunk = min(4, per_half)

    def project(h):
        for c in range(per_half // chunk):
            rays = chunk * LANES
            cells = []
            for q in range(c * chunk, (c + 1) * chunk):
                sample_loads[h * per_half + q].wait()
                start = (HALVES * q + h) * group_rows
                cells.append(samples_ref[start : start + group_rows].reshape(LANES, K * F))
            x = jnp.concatenate(cells, axis=0)
            for pair in range(K // 2):
                part = x[:, pair * LANES : (pair + 1) * LANES].astype(BF16)
                act = jnp.maximum(dot(part, pair_w) + pair_b, 0.0).astype(BF16)
                for half in range(2):
                    k = 2 * pair + half
                    out = dot(act[:, half * hid : (half + 1) * hid], heads)
                    color = (out[:, :channels] + b_color).astype(BF16)
                    before = out[:, channels:].reshape(chunk, LANES, LANES)
                    for q in range(chunk):
                        colors_ref[h, c * chunk + q, k * LANES : (k + 1) * LANES, :] = color[
                            q * LANES : (q + 1) * LANES
                        ]
                    density_ref[h, k, c * chunk : (c + 1) * chunk, :] = jnp.sum(
                        jnp.where(eye, before, 0.0), axis=1
                    )

    def send_depth(h):
        density = []
        for k in range(K):
            z = density_ref[h, k] + b_density_ref[0]
            soft = jnp.maximum(z, 0.0) + jnp.log1p(jnp.exp(-jnp.abs(z)))
            density.append(jnp.where(live[h] > k, soft, 0.0))
        depths_ref[h, me] = density[0] + density[1] + density[2] + density[3]
        if h == 0:
            pl.semaphore_wait(
                barrier, slabs + not_first.astype(jnp.int32) + not_last.astype(jnp.int32)
            )

        def send(shift, carry):
            pltpu.make_async_remote_copy(
                src_ref=depths_ref.at[h, me],
                dst_ref=depths_ref.at[h, me],
                send_sem=depth_send.at[h],
                recv_sem=depth_recv.at[h],
                device_id=(lax.rem(me + shift, slabs), tile),
                device_id_type=MESH,
            ).start()
            return carry

        lax.fori_loop(1, slabs, send, 0)
        return density

    def weigh(h, density):
        peers = depths_ref.at[h, pl.ds(0, slabs - 1)]
        pltpu.make_async_copy(peers, peers, depth_recv.at[h]).wait()
        total = depths_ref[h, 0]
        prefix = jnp.where(me > 0, total, 0.0)
        for s in range(1, slabs):
            one = depths_ref[h, s]
            total = total + one
            prefix = prefix + jnp.where(s < me, one, 0.0)
        front = prefix / total
        ahead = front
        for k in range(K):
            scaled = density[k] / total
            weight_ref[h, k] = jnp.exp(-ahead) * (1.0 - jnp.exp(-scaled))
            ahead = ahead + scaled
        return front

    def send_part(owner):
        pltpu.make_async_remote_copy(
            src_ref=sent_ref.at[owner],
            dst_ref=parts_ref.at[me],
            send_sem=part_send,
            recv_sem=part_recv,
            device_id=(owner, tile),
            device_id_type=MESH,
        ).start()

    strips = LANES // strip_rays

    def scatter(h):
        for i in range(per_half):
            q = lax.rem(me // (strips * HALVES) + i, per_half)
            diag = [
                jnp.where(eye, weight_ref[h, k, pl.ds(q, 1), :], 0.0).astype(BF16)
                for k in range(K)
            ]
            image = dot(jnp.concatenate(diag, axis=1), colors_ref[h, q]).astype(BF16)
            first = strips * (HALVES * q + h)
            sent_ref[pl.ds(first, strips)] = image.reshape(strips, strip_rays, channels)
            for j in range(strips):
                owner = first + j
                if i > 0:
                    send_part(owner)
                else:
                    pl.when(owner != me)(functools.partial(send_part, owner))

    project(0)

    for load in last_loads:
        load.wait()
    spread = (
        lax.rem(lax.broadcasted_iota(jnp.int32, (cols, LANES), 1), cols)
        == lax.broadcasted_iota(jnp.int32, (cols, LANES), 0)
    ).astype(BF16)
    own_lane = (
        lax.broadcasted_iota(jnp.int32, (group_rows, LANES), 1) // cols
        == lax.broadcasted_iota(jnp.int32, (group_rows, LANES), 0)
    )
    row_eye = (
        lax.broadcasted_iota(jnp.int32, (rows, rows), 0)
        == lax.broadcasted_iota(jnp.int32, (rows, rows), 1)
    ).astype(BF16)
    by_row = dot_last(row_eye, counts_ref[...].astype(F32).astype(BF16)).astype(BF16)
    spread_counts = dot(by_row, spread).reshape(per_half, HALVES, group_rows, LANES)
    live = [
        jnp.sum(jnp.where(own_lane, spread_counts[:, h], 0.0), axis=1) for h in range(HALVES)
    ]

    densities = [send_depth(0)]
    for h in range(1, HALVES):
        project(h)
        densities.append(send_depth(h))
    fronts = []
    for h in range(HALVES):
        fronts.append(weigh(h, densities[h]))
        scatter(h)
    parts_ref[me] = sent_ref[me]

    for taps, conv in ((taps_a, conv_a_ref), (taps_b, conv_b_ref)):
        for r in range(3):
            for s in range(3):
                taps[r * channels : (r + 1) * channels, s * channels : (s + 1) * channels] = conv[
                    r, s
                ]

    laid = jnp.stack(
        [jnp.where(own_lane, front[:, None, :], 0.0) for front in fronts], axis=1
    ).reshape(rows, LANES)
    first = laid.astype(BF16)
    rest = laid - first.astype(F32)
    second = rest.astype(BF16)
    third = (rest - second.astype(F32)).astype(BF16)
    front_ref[0] = dot_last(spread, first) + dot_last(spread, second) + dot_last(spread, third)

    peers = parts_ref.at[pl.ds(0, slabs - 1)]
    pltpu.make_async_copy(peers, peers, part_recv).wait()
    image = parts_ref[0].astype(F32)
    for s in range(1, slabs):
        image = image + parts_ref[s].astype(F32)
    image = image.astype(BF16).reshape(strip, cols, channels)

    field_ref[0, 2 : 2 + strip] = image
    edge = jnp.zeros((2, 2, cols, channels), BF16)

    def edge_copy(which, source, target, device):
        return pltpu.make_async_remote_copy(
            src_ref=source,
            dst_ref=target,
            send_sem=edge_send.at[which],
            recv_sem=edge_recv.at[which],
            device_id=device,
            device_id_type=MESH,
        )

    own = field_ref.at[0, pl.ds(2, strip)]
    head = field_ref.at[0, pl.ds(2, 2)]
    tail = field_ref.at[0, pl.ds(strip, 2)]
    up = [
        edge_copy(1, head, field_ref.at[0, pl.ds(strip + 2, 2)], (me - 1, tile)),
        edge_copy(2, head, field_ref.at[1, pl.ds(strip + 2, 2)], (me - 1, other)),
    ]
    down = [
        edge_copy(3, tail, field_ref.at[0, pl.ds(0, 2)], (me + 1, tile)),
        edge_copy(4, tail, field_ref.at[1, pl.ds(0, 2)], (me + 1, other)),
    ]
    across = edge_copy(0, own, field_ref.at[1, pl.ds(2, strip)], (me, other))

    @pl.when(not_first)
    def _():
        for copy in up:
            copy.start()

    @pl.when(not_last)
    def _():
        for copy in down:
            copy.start()

    across.start()

    @pl.when(jnp.logical_not(not_first))
    def _():
        field_ref[:, 0:2] = edge

    @pl.when(jnp.logical_not(not_last))
    def _():
        field_ref[:, strip + 2 : strip + 4] = edge

    @pl.when(not_last)
    def _():
        for copy in up:
            copy.wait_recv()

    @pl.when(not_first)
    def _():
        for copy in down:
            copy.wait_recv()

    across.wait_recv()

    place = lax.broadcasted_iota(jnp.int32, (1, cols, 1), 1)
    near = jnp.where(tile == 0, place, cols - 1 - place) < 2
    side = jnp.where(near, field_ref[1].astype(F32), 0.0).astype(BF16)
    ring = jnp.concatenate([field_ref[0], side], axis=1)

    def convolve(cells, taps, bias):
        out_rows = cells.shape[0] - 2
        span = cells.shape[1]
        stacked = jnp.concatenate(
            [cells[r : r + out_rows].reshape(out_rows * span, channels) for r in range(3)], axis=1
        )
        shifted = dot(stacked, taps[...]).reshape(out_rows, span, 3 * channels)
        return (
            pltpu.roll(shifted[:, :, :channels], 1, 1)
            + shifted[:, :, channels : 2 * channels]
            + pltpu.roll(shifted[:, :, 2 * channels :], span - 1, 1)
            + bias
        )

    hidden_map = jnp.maximum(convolve(ring, taps_a, bias_a_ref[...].reshape(1, 1, channels)), 0.0)
    shape = (strip + 2, 2 * cols, 1)
    at_row = lax.broadcasted_iota(jnp.int32, shape, 0) + me * strip - 1
    at_col = lax.broadcasted_iota(jnp.int32, shape, 1)
    in_rows = jnp.logical_and(at_row >= 0, at_row < rows)
    outside = jnp.where(tile == 0, 2 * cols - 1, cols)
    hidden_map = jnp.where(jnp.logical_and(in_rows, at_col != outside), hidden_map, 0.0)
    decoded = convolve(hidden_map.astype(BF16), taps_b, bias_b_ref[...].reshape(1, 1, channels))
    decoded_ref[...] = decoded[:, :cols].astype(BF16)

    for h in range(HALVES):
        peers = depths_ref.at[h, pl.ds(0, slabs - 1)]
        pltpu.make_async_copy(peers, peers, depth_send.at[h]).wait()
    peers = parts_ref.at[pl.ds(0, slabs - 1)]
    pltpu.make_async_copy(peers, peers, part_send).wait()
    across.wait_send()

    @pl.when(not_first)
    def _():
        for copy in up:
            copy.wait_send()

    @pl.when(not_last)
    def _():
        for copy in down:
            copy.wait_send()


def stay(array):
    return pltpu.with_memory_space_constraint(array, pltpu.HBM)


def body(
    slabs,
    samples,
    counts,
    w_in,
    b_in,
    w_color,
    b_color,
    w_density,
    b_density,
    conv_a,
    bias_a,
    conv_b,
    bias_b,
):
    _, rows, cols, width = samples.shape
    hid, channels = w_color.shape[1:]
    groups = rows * cols // LANES
    strip = rows // slabs
    vmem = pl.BlockSpec(memory_space=pltpu.VMEM)
    smem = pl.BlockSpec(memory_space=pltpu.SMEM)
    hbm = pl.BlockSpec(memory_space=pltpu.HBM)
    dma = pltpu.SemaphoreType.DMA
    per_half = groups // HALVES
    decoded, front = pl.pallas_call(
        functools.partial(render_kernel, slabs),
        out_shape=(
            jax.ShapeDtypeStruct((strip, cols, channels), BF16),
            jax.ShapeDtypeStruct((1, cols, rows), F32),
        ),
        in_specs=[hbm] * 7 + [smem] + [hbm] * 4,
        out_specs=(vmem, vmem),
        scratch_shapes=[
            pltpu.VMEM((rows, cols, width), F32),
            pltpu.VMEM((cols, rows), jnp.int32),
            pltpu.VMEM(w_in.shape[1:], F32),
            pltpu.VMEM((1, hid), F32),
            pltpu.VMEM(w_color.shape[1:], F32),
            pltpu.VMEM((1, channels), F32),
            pltpu.VMEM((1, hid), F32),
            pltpu.VMEM(conv_a.shape, BF16),
            pltpu.VMEM((1, channels), F32),
            pltpu.VMEM(conv_b.shape, BF16),
            pltpu.VMEM((1, channels), F32),
            pltpu.VMEM((3 * channels, 3 * channels), BF16),
            pltpu.VMEM((3 * channels, 3 * channels), BF16),
            pltpu.VMEM((HALVES, K, per_half, LANES), F32),
            pltpu.VMEM((HALVES, per_half, K * LANES, channels), BF16),
            pltpu.VMEM((HALVES, K, per_half, LANES), F32),
            pltpu.VMEM((HALVES, slabs, per_half, LANES), F32),
            pltpu.VMEM((slabs, strip * cols, channels), BF16),
            pltpu.VMEM((slabs, strip * cols, channels), BF16),
            pltpu.VMEM((2, strip + 4, cols, channels), BF16),
            dma((10 + groups,)),
            dma((HALVES,)),
            dma((HALVES,)),
            dma,
            dma,
            dma((5,)),
            dma((5,)),
        ],
        compiler_params=pltpu.CompilerParams(
            collective_id=0, has_side_effects=True, vmem_limit_bytes=32 * 2**20
        ),
    )(
        stay(samples),
        stay(jnp.swapaxes(counts, 1, 2)),
        stay(w_in),
        stay(b_in),
        stay(w_color),
        stay(b_color),
        stay(w_density),
        b_density,
        stay(conv_a),
        stay(bias_a.reshape(1, channels)),
        stay(conv_b),
        stay(bias_b.reshape(1, channels)),
    )
    return decoded, jnp.swapaxes(front, 1, 2)


def solution(mesh):
    in_specs = (
        P("slab", None, "tile", None),
        P("slab", None, "tile"),
        P("slab", None, None),
        P("slab", None),
        P("slab", None, None),
        P("slab", None),
        P("slab", None),
        P("slab"),
        P(),
        P(),
        P(),
        P(),
    )
    out_specs = (P("slab", "tile", None), P("slab", None, "tile"))
    run = functools.partial(body, mesh.shape["slab"])
    return jax.shard_map(run, mesh=mesh, in_specs=in_specs, out_specs=out_specs, check_vma=False)
```

```python
import functools

import jax
import jax.numpy as jnp
from jax import lax
from jax.experimental import pallas as pl
from jax.experimental.pallas import tpu as pltpu
from jax.sharding import PartitionSpec as P

F = 64
K = 4
LANES = 128
HALVES = 2
MESH = pl.DeviceIdType.MESH
BF16 = jnp.bfloat16
F32 = jnp.float32


def dot(a, b):
    return jnp.dot(a, b, preferred_element_type=F32)


def dot_last(a, b):
    return lax.dot_general(a, b, (((1,), (1,)), ((), ())), preferred_element_type=F32)


def render_kernel(
    slabs,
    samples_hbm,
    counts_hbm,
    w_in_hbm,
    b_in_hbm,
    w_color_hbm,
    b_color_hbm,
    w_density_hbm,
    b_density_ref,
    conv_a_hbm,
    bias_a_hbm,
    conv_b_hbm,
    bias_b_hbm,
    decoded_ref,
    front_ref,
    samples_ref,
    counts_ref,
    w_in_ref,
    b_in_ref,
    w_color_ref,
    b_color_ref,
    w_density_ref,
    conv_a_ref,
    bias_a_ref,
    conv_b_ref,
    bias_b_ref,
    taps_a,
    taps_b,
    density_ref,
    colors_ref,
    weight_ref,
    depths_ref,
    sent_ref,
    parts_ref,
    field_ref,
    load_sems,
    depth_send,
    depth_recv,
    part_send,
    part_recv,
    edge_send,
    edge_recv,
):
    me = lax.axis_index("slab")
    tile = lax.axis_index("tile")
    other = 1 - tile
    rows, cols = samples_ref.shape[0], samples_ref.shape[1]
    groups = rows * cols // LANES
    group_rows = LANES // cols
    strip = rows // slabs
    strip_rays = strip * cols
    hid = w_in_ref.shape[1]
    channels = w_color_ref.shape[1]
    not_first = me > 0
    not_last = me < slabs - 1

    per_half = groups // HALVES
    order = [HALVES * q + h for h in range(HALVES) for q in range(per_half)]
    pieces = [pl.ds(g * group_rows, group_rows) for g in order]
    first_loads = [
        (w_in_hbm.at[0], w_in_ref),
        (b_in_hbm, b_in_ref),
        (counts_hbm.at[0], counts_ref),
        (w_color_hbm.at[0], w_color_ref),
        (w_density_hbm, w_density_ref),
        (b_color_hbm, b_color_ref),
    ]
    last_loads = [
        (conv_a_hbm, conv_a_ref),
        (conv_b_hbm, conv_b_ref),
        (bias_a_hbm, bias_a_ref),
        (bias_b_hbm, bias_b_ref),
    ]
    sample_loads = [(samples_hbm.at[0, piece], samples_ref.at[piece]) for piece in pieces]
    loads = [
        pltpu.make_async_copy(src, dst, load_sems.at[i])
        for i, (src, dst) in enumerate(first_loads + last_loads + sample_loads)
    ]
    sample_loads = loads[len(first_loads) + len(last_loads) :]
    last_loads = loads[len(first_loads) : len(first_loads) + len(last_loads)]
    first_loads = loads[: len(first_loads)]
    for load in first_loads + sample_loads + last_loads:
        load.start()

    barrier = pltpu.get_barrier_semaphore()

    def greet(slab, tile_at):
        pl.semaphore_signal(barrier, inc=1, device_id=(slab, tile_at), device_id_type=MESH)

    for shift in range(1, slabs):
        greet(lax.rem(me + shift, slabs), tile)
    greet(me, other)

    @pl.when(not_first)
    def _():
        greet(me - 1, other)

    @pl.when(not_last)
    def _():
        greet(me + 1, other)

    eye = lax.broadcasted_iota(jnp.int32, (LANES, LANES), 0) == lax.broadcasted_iota(
        jnp.int32, (LANES, LANES), 1
    )

    for load in first_loads:
        load.wait()
    w_in = w_in_ref[...].astype(BF16)
    blank = jnp.zeros_like(w_in)
    pair_w = jnp.concatenate(
        [jnp.concatenate([w_in, blank], axis=0), jnp.concatenate([blank, w_in], axis=0)], axis=1
    )
    pair_b = jnp.concatenate([b_in_ref[...], b_in_ref[...]], axis=1)
    density_cols = jnp.transpose(jnp.broadcast_to(w_density_ref[...], (LANES, hid)))
    heads = jnp.concatenate([w_color_ref[...].astype(BF16), density_cols.astype(BF16)], axis=1)
    b_color = b_color_ref[...]
    chunk = min(4, per_half)

    def project(h):
        for c in range(per_half // chunk):
            rays = chunk * LANES
            cells = []
            for q in range(c * chunk, (c + 1) * chunk):
                sample_loads[h * per_half + q].wait()
                start = (HALVES * q + h) * group_rows
                cells.append(samples_ref[start : start + group_rows].reshape(LANES, K * F))
            x = jnp.concatenate(cells, axis=0)
            for pair in range(K // 2):
                part = x[:, pair * LANES : (pair + 1) * LANES].astype(BF16)
                act = jnp.maximum(dot(part, pair_w) + pair_b, 0.0).astype(BF16)
                for half in range(2):
                    k = 2 * pair + half
                    out = dot(act[:, half * hid : (half + 1) * hid], heads)
                    color = (out[:, :channels] + b_color).astype(BF16)
                    before = out[:, channels:].reshape(chunk, LANES, LANES)
                    for q in range(chunk):
                        colors_ref[h, c * chunk + q, k * LANES : (k + 1) * LANES, :] = color[
                            q * LANES : (q + 1) * LANES
                        ]
                    density_ref[h, k, c * chunk : (c + 1) * chunk, :] = jnp.sum(
                        jnp.where(eye, before, 0.0), axis=1
                    )

    def send_depth(h):
        density = []
        for k in range(K):
            z = density_ref[h, k] + b_density_ref[0]
            soft = jnp.maximum(z, 0.0) + jnp.log1p(jnp.exp(-jnp.abs(z)))
            density.append(jnp.where(live[h] > k, soft, 0.0))
        depths_ref[h, me] = density[0] + density[1] + density[2] + density[3]
        if h == 0:
            pl.semaphore_wait(
                barrier, slabs + not_first.astype(jnp.int32) + not_last.astype(jnp.int32)
            )

        for shift in range(1, slabs):
            pltpu.make_async_remote_copy(
                src_ref=depths_ref.at[h, me],
                dst_ref=depths_ref.at[h, me],
                send_sem=depth_send.at[h],
                recv_sem=depth_recv.at[h],
                device_id=(lax.rem(me + shift, slabs), tile),
                device_id_type=MESH,
            ).start()
        return density

    def weigh(h, density):
        peers = depths_ref.at[h, pl.ds(0, slabs - 1)]
        pltpu.make_async_copy(peers, peers, depth_recv.at[h]).wait()
        total = depths_ref[h, 0]
        prefix = jnp.where(me > 0, total, 0.0)
        for s in range(1, slabs):
            one = depths_ref[h, s]
            total = total + one
            prefix = prefix + jnp.where(s < me, one, 0.0)
        front = prefix / total
        ahead = front
        for k in range(K):
            scaled = density[k] / total
            weight_ref[h, k] = jnp.exp(-ahead) * (1.0 - jnp.exp(-scaled))
            ahead = ahead + scaled
        return front

    def send_part(owner):
        pltpu.make_async_remote_copy(
            src_ref=sent_ref.at[owner],
            dst_ref=parts_ref.at[me],
            send_sem=part_send,
            recv_sem=part_recv,
            device_id=(owner, tile),
            device_id_type=MESH,
        ).start()

    strips = LANES // strip_rays

    def scatter(h):
        for i in range(per_half):
            q = lax.rem(me // (strips * HALVES) + i, per_half)
            diag = [
                jnp.where(eye, weight_ref[h, k, pl.ds(q, 1), :], 0.0).astype(BF16)
                for k in range(K)
            ]
            image = dot(jnp.concatenate(diag, axis=1), colors_ref[h, q]).astype(BF16)
            first = strips * (HALVES * q + h)
            sent_ref[pl.ds(first, strips)] = image.reshape(strips, strip_rays, channels)
            for j in range(strips):
                owner = first + j
                if i > 0:
                    send_part(owner)
                else:
                    pl.when(owner != me)(functools.partial(send_part, owner))

    spread = (
        lax.rem(lax.broadcasted_iota(jnp.int32, (cols, LANES), 1), cols)
        == lax.broadcasted_iota(jnp.int32, (cols, LANES), 0)
    ).astype(BF16)
    own_lane = (
        lax.broadcasted_iota(jnp.int32, (group_rows, LANES), 1) // cols
        == lax.broadcasted_iota(jnp.int32, (group_rows, LANES), 0)
    )
    row_eye = (
        lax.broadcasted_iota(jnp.int32, (rows, rows), 0)
        == lax.broadcasted_iota(jnp.int32, (rows, rows), 1)
    ).astype(BF16)
    by_row = dot_last(row_eye, counts_ref[...].astype(F32).astype(BF16)).astype(BF16)
    spread_counts = dot(by_row, spread).reshape(per_half, HALVES, group_rows, LANES)
    live = [
        jnp.sum(jnp.where(own_lane, spread_counts[:, h], 0.0), axis=1) for h in range(HALVES)
    ]

    project(0)
    densities = [send_depth(0)]
    for h in range(1, HALVES):
        project(h)
        densities.append(send_depth(h))
    fronts = []
    for h in range(HALVES):
        fronts.append(weigh(h, densities[h]))
        scatter(h)
    parts_ref[me] = sent_ref[me]

    for load in last_loads:
        load.wait()
    for taps, conv in ((taps_a, conv_a_ref), (taps_b, conv_b_ref)):
        for r in range(3):
            for s in range(3):
                taps[r * channels : (r + 1) * channels, s * channels : (s + 1) * channels] = conv[
                    r, s
                ]

    laid = jnp.stack(
        [jnp.where(own_lane, front[:, None, :], 0.0) for front in fronts], axis=1
    ).reshape(rows, LANES)
    first = laid.astype(BF16)
    rest = laid - first.astype(F32)
    second = rest.astype(BF16)
    third = (rest - second.astype(F32)).astype(BF16)
    front_ref[0] = dot_last(spread, first) + dot_last(spread, second) + dot_last(spread, third)

    peers = parts_ref.at[pl.ds(0, slabs - 1)]
    pltpu.make_async_copy(peers, peers, part_recv).wait()
    image = parts_ref[0].astype(F32)
    for s in range(1, slabs):
        image = image + parts_ref[s].astype(F32)
    image = image.astype(BF16).reshape(strip, cols, channels)

    field_ref[0, 2 : 2 + strip] = image
    edge = jnp.zeros((2, 2, cols, channels), BF16)

    def edge_copy(which, source, target, device):
        return pltpu.make_async_remote_copy(
            src_ref=source,
            dst_ref=target,
            send_sem=edge_send.at[which],
            recv_sem=edge_recv.at[which],
            device_id=device,
            device_id_type=MESH,
        )

    own = field_ref.at[0, pl.ds(2, strip)]
    head = field_ref.at[0, pl.ds(2, 2)]
    tail = field_ref.at[0, pl.ds(strip, 2)]
    up = [
        edge_copy(1, head, field_ref.at[0, pl.ds(strip + 2, 2)], (me - 1, tile)),
        edge_copy(2, head, field_ref.at[1, pl.ds(strip + 2, 2)], (me - 1, other)),
    ]
    down = [
        edge_copy(3, tail, field_ref.at[0, pl.ds(0, 2)], (me + 1, tile)),
        edge_copy(4, tail, field_ref.at[1, pl.ds(0, 2)], (me + 1, other)),
    ]
    across = edge_copy(0, own, field_ref.at[1, pl.ds(2, strip)], (me, other))

    @pl.when(not_first)
    def _():
        for copy in up:
            copy.start()

    @pl.when(not_last)
    def _():
        for copy in down:
            copy.start()

    across.start()

    @pl.when(jnp.logical_not(not_first))
    def _():
        field_ref[:, 0:2] = edge

    @pl.when(jnp.logical_not(not_last))
    def _():
        field_ref[:, strip + 2 : strip + 4] = edge

    @pl.when(not_last)
    def _():
        for copy in up:
            copy.wait_recv()

    @pl.when(not_first)
    def _():
        for copy in down:
            copy.wait_recv()

    across.wait_recv()

    place = lax.broadcasted_iota(jnp.int32, (1, cols, 1), 1)
    near = jnp.where(tile == 0, place, cols - 1 - place) < 2
    side = jnp.where(near, field_ref[1].astype(F32), 0.0).astype(BF16)
    ring = jnp.concatenate([field_ref[0], side], axis=1)

    def convolve(cells, taps, bias):
        out_rows = cells.shape[0] - 2
        span = cells.shape[1]
        stacked = jnp.concatenate(
            [cells[r : r + out_rows].reshape(out_rows * span, channels) for r in range(3)], axis=1
        )
        shifted = dot(stacked, taps[...]).reshape(out_rows, span, 3 * channels)
        return (
            pltpu.roll(shifted[:, :, :channels], 1, 1)
            + shifted[:, :, channels : 2 * channels]
            + pltpu.roll(shifted[:, :, 2 * channels :], span - 1, 1)
            + bias
        )

    hidden_map = jnp.maximum(convolve(ring, taps_a, bias_a_ref[...].reshape(1, 1, channels)), 0.0)
    shape = (strip + 2, 2 * cols, 1)
    at_row = lax.broadcasted_iota(jnp.int32, shape, 0) + me * strip - 1
    at_col = lax.broadcasted_iota(jnp.int32, shape, 1)
    in_rows = jnp.logical_and(at_row >= 0, at_row < rows)
    outside = jnp.where(tile == 0, 2 * cols - 1, cols)
    hidden_map = jnp.where(jnp.logical_and(in_rows, at_col != outside), hidden_map, 0.0)
    decoded = convolve(hidden_map.astype(BF16), taps_b, bias_b_ref[...].reshape(1, 1, channels))
    decoded_ref[...] = decoded[:, :cols].astype(BF16)

    for h in range(HALVES):
        peers = depths_ref.at[h, pl.ds(0, slabs - 1)]
        pltpu.make_async_copy(peers, peers, depth_send.at[h]).wait()
    peers = parts_ref.at[pl.ds(0, slabs - 1)]
    pltpu.make_async_copy(peers, peers, part_send).wait()
    across.wait_send()

    @pl.when(not_first)
    def _():
        for copy in up:
            copy.wait_send()

    @pl.when(not_last)
    def _():
        for copy in down:
            copy.wait_send()


def stay(array):
    return pltpu.with_memory_space_constraint(array, pltpu.HBM)


def body(
    slabs,
    samples,
    counts,
    w_in,
    b_in,
    w_color,
    b_color,
    w_density,
    b_density,
    conv_a,
    bias_a,
    conv_b,
    bias_b,
):
    _, rows, cols, width = samples.shape
    hid, channels = w_color.shape[1:]
    groups = rows * cols // LANES
    strip = rows // slabs
    vmem = pl.BlockSpec(memory_space=pltpu.VMEM)
    smem = pl.BlockSpec(memory_space=pltpu.SMEM)
    hbm = pl.BlockSpec(memory_space=pltpu.HBM)
    dma = pltpu.SemaphoreType.DMA
    per_half = groups // HALVES
    decoded, front = pl.pallas_call(
        functools.partial(render_kernel, slabs),
        out_shape=(
            jax.ShapeDtypeStruct((strip, cols, channels), BF16),
            jax.ShapeDtypeStruct((1, cols, rows), F32),
        ),
        in_specs=[hbm] * 7 + [smem] + [hbm] * 4,
        out_specs=(vmem, vmem),
        scratch_shapes=[
            pltpu.VMEM((rows, cols, width), F32),
            pltpu.VMEM((cols, rows), jnp.int32),
            pltpu.VMEM(w_in.shape[1:], F32),
            pltpu.VMEM((1, hid), F32),
            pltpu.VMEM(w_color.shape[1:], F32),
            pltpu.VMEM((1, channels), F32),
            pltpu.VMEM((1, hid), F32),
            pltpu.VMEM(conv_a.shape, BF16),
            pltpu.VMEM((1, channels), F32),
            pltpu.VMEM(conv_b.shape, BF16),
            pltpu.VMEM((1, channels), F32),
            pltpu.VMEM((3 * channels, 3 * channels), BF16),
            pltpu.VMEM((3 * channels, 3 * channels), BF16),
            pltpu.VMEM((HALVES, K, per_half, LANES), F32),
            pltpu.VMEM((HALVES, per_half, K * LANES, channels), BF16),
            pltpu.VMEM((HALVES, K, per_half, LANES), F32),
            pltpu.VMEM((HALVES, slabs, per_half, LANES), F32),
            pltpu.VMEM((slabs, strip * cols, channels), BF16),
            pltpu.VMEM((slabs, strip * cols, channels), BF16),
            pltpu.VMEM((2, strip + 4, cols, channels), BF16),
            dma((10 + groups,)),
            dma((HALVES,)),
            dma((HALVES,)),
            dma,
            dma,
            dma((5,)),
            dma((5,)),
        ],
        compiler_params=pltpu.CompilerParams(
            collective_id=0, has_side_effects=True, vmem_limit_bytes=32 * 2**20
        ),
    )(
        stay(samples),
        stay(jnp.swapaxes(counts, 1, 2)),
        stay(w_in),
        stay(b_in),
        stay(w_color),
        stay(b_color),
        stay(w_density),
        b_density,
        stay(conv_a),
        stay(bias_a.reshape(1, channels)),
        stay(conv_b),
        stay(bias_b.reshape(1, channels)),
    )
    return decoded, jnp.swapaxes(front, 1, 2)


def solution(mesh):
    in_specs = (
        P("slab", None, "tile", None),
        P("slab", None, "tile"),
        P("slab", None, None),
        P("slab", None),
        P("slab", None, None),
        P("slab", None),
        P("slab", None),
        P("slab"),
        P(),
        P(),
        P(),
        P(),
    )
    out_specs = (P("slab", "tile", None), P("slab", None, "tile"))
    run = functools.partial(body, mesh.shape["slab"])
    return jax.shard_map(run, mesh=mesh, in_specs=in_specs, out_specs=out_specs, check_vma=False)
```
